32 devices in a mesh: grp: 2 (over y), slab: 4 (over z), coil: 2 (over x), half: 2 (over core).
Axes of the slice: x: 2, y: 2, z: 4, core: 2. Of those that a mesh axis runs over, the one named last changes fastest.
Arguments:
- kspace: bfloat16 [32, 4, 128, 640], P(('grp', 'coil', 'half'), None, 'slab'), parts along dimension 0, may hold values from -6 to 6
- measured: bfloat16 [32, 4, 128, 640], P(('grp', 'coil', 'half'), None, 'slab'), parts along dimension 0, may hold values from -6 to 6
- cotangent: bfloat16 [32, 4, 128, 640], P(('grp', 'coil', 'half'), None, 'slab'), parts along dimension 0, may hold values from -0.014770508 to 0.014770508
- coil_maps: bfloat16 [32, 4, 128, 640], P(('grp', 'coil', 'half'), 'slab'), parts along dimension 0, may hold values from -3 to 3
- sample_mask: int32 [256, 320], P(('grp', 'slab')), parts along dimension 0, may hold values 0 or 1
- step_size: float32 [1], replicated, may hold values from 0.5 to 1.5
- weight_first: bfloat16 [3, 3, 32, 3, 2], replicated, may hold values from -0.875 to 0.875
- weight_middle: bfloat16 [3, 3, 32, 3, 32], replicated, may hold values from -0.21875 to 0.21875
- weight_last: bfloat16 [3, 3, 2, 3, 32], replicated, may hold values from -0.21875 to 0.21875
Outputs:
- updated: bfloat16 [32, 4, 128, 640], P(('grp', 'coil', 'half'), None, 'slab'), parts along dimension 0
- grad_first: float32 [6, 3, 32, 3, 2], P('grp'), parts along dimension 0
- grad_middle: float32 [6, 3, 32, 3, 32], P('grp'), parts along dimension 0
- grad_last: float32 [6, 3, 2, 3, 32], P('grp'), parts along dimension 0
The draws below stay inside these ranges and needn't reach their ends.
There are 2 independent parts, one for each index of `grp`. The reference program is written for one: setup_inputs(seed, part) draws one part's arguments, and reference() takes and returns one part's arrays. A program takes and returns all parts, laid end to end along the dimension named above; an argument that names none is the same for every part. Nothing has to cross between parts.
Inputs may be any that keep to these rules, and one draw needn't show every extreme that they name: `sample_mask`: 1 where the phase-encode line (kz, ky) was acquired.
All inputs are finite; a program needn't handle non-finite values. No bound on the sum of `sample_mask` on one device may be relied on, other than what follows from the above.
Results may differ from the reference program's by a relative error of at most 0.0091.
Values may be sent and summed in bfloat16 or wider, within the bound.
A program may use at most 64 MiB of HBM per device.

```python
import jax
import jax.numpy as jnp
from jax import lax

NC = 16
NY = 320
NZ = 128
CH = 32
XW = 4


def touch_ends(entries, rng, smallest, high):
    spot = [jax.random.randint(jax.random.fold_in(rng, axis), (), 0, length) for axis, length in enumerate(entries.shape)]
    main_axis = entries.shape.index(max(entries.shape))
    neighbour = spot[:main_axis] + [(spot[main_axis] + 1) % entries.shape[main_axis]] + spot[main_axis + 1:]
    return entries.at[tuple(spot)].set(smallest).at[tuple(neighbour)].set(high)


def block_levels(stream_key, shape, split, low, high):
    level, own = 1.0, jax.random.fold_in(stream_key, 6)
    for axis_at, shards_of in split:
        draws = jnp.exp(jax.random.uniform(jax.random.fold_in(own, axis_at), (shards_of,), jnp.float32, low / len(split), high / len(split)))
        level = level * jnp.repeat(draws, shape[axis_at] // shards_of).reshape([-1 if axis == axis_at else 1 for axis in range(len(shape))])
    return level


def noise(rng, extent, width, most, pieces=(), dtype=jnp.bfloat16):
    result = width * jax.random.normal(rng, extent, jnp.float32)
    if pieces:
        result = result * block_levels(rng, extent, pieces, -0.22, 0.18)
    return jnp.clip(result, -most, most).astype(dtype)


def setup_inputs(seed: int = 0, part: int = 0) -> dict:
    seeds = jax.random.split(jax.random.key(seed), 10)
    part_keys = jax.random.split(jax.random.fold_in(seeds[9], part), 10)
    kspace = noise(part_keys[0], (NC, XW, NZ, 2 * NY), 1.0, 6.0, ((0, 4), (2, 4)))
    measured = noise(part_keys[1], (NC, XW, NZ, 2 * NY), 1.0, 6.0, ((0, 4), (2, 4)))
    cotangent = noise(part_keys[2], (NC, XW, NZ, 2 * NY), (1.0 / (XW * NZ * NY) ** 0.5), 0.014770508, ((0, 4), (2, 4)))
    coil_maps = noise(part_keys[3], (NC, XW, NZ, 2 * NY), 0.5, 3.0, ((0, 4), (1, 4)))
    sample_mask = touch_ends((jax.random.randint(part_keys[4], (NZ, NY), 0, 3) < 1).astype(jnp.int32), jax.random.fold_in(part_keys[4], 1), 0, 1)
    step_size = jnp.clip(jax.random.uniform(seeds[5], (1,), jnp.float32, 0.5, 1.5), 0.5, 1.5)
    weight_first = noise(seeds[6], (3, 3, CH, 3, 2), 54 ** -0.5, 0.875)
    weight_middle = noise(seeds[7], (3, 3, CH, 3, CH), (27 * CH) ** -0.5, 0.21875)
    weight_last = noise(seeds[8], (3, 3, 2, 3, CH), (27 * CH) ** -0.5, 0.21875)
    return {"kspace": kspace, "measured": measured, "cotangent": cotangent, "coil_maps": coil_maps, "sample_mask": sample_mask, "step_size": step_size, "weight_first": weight_first, "weight_middle": weight_middle, "weight_last": weight_last}


def to_complex(values):
    half_len = values.shape[-1] // 2
    wide = values.astype(jnp.float32)
    return lax.complex(wide[..., :half_len], wide[..., half_len:])

def coil_adjoint(kdata, coil_maps):
    images = jnp.fft.ifftn(to_complex(kdata), axes=(2, 3), norm='ortho')
    summed = lax.optimization_barrier(jnp.sum(jnp.conj(to_complex(coil_maps)) * images, axis=0))
    return jnp.stack([jnp.real(summed), jnp.imag(summed)], axis=2)

def conv_layer(inputs, weight):
    return lax.conv_general_dilated(inputs[None], weight, (1, 1, 1), [(1, 1), (1, 1), (1, 1)], dimension_numbers=('NDHCW', 'DHOWI', 'NDHCW'), precision=lax.Precision.HIGHEST)[0]

def silu_grad(values):
    sigma = jax.nn.sigmoid(values)
    return sigma * (1.0 + values * (1.0 - sigma))

def pull_back(inputs, weight, incoming):
    _, puller = jax.vjp(conv_layer, inputs.astype(jnp.float32), weight.astype(jnp.float32))
    return puller(incoming.astype(jnp.float32))

def reference(kspace, measured, cotangent, coil_maps, sample_mask, step_size, weight_first, weight_middle, weight_last):
    image = coil_adjoint(kspace, coil_maps)
    layer_zero = image.astype(jnp.bfloat16)
    pre_first = conv_layer(layer_zero.astype(jnp.float32), weight_first.astype(jnp.float32))
    act_first = jax.nn.silu(pre_first).astype(jnp.bfloat16)
    pre_middle = conv_layer(act_first.astype(jnp.float32), weight_middle.astype(jnp.float32))
    act_middle = jax.nn.silu(pre_middle).astype(jnp.bfloat16)
    refined = conv_layer(act_middle.astype(jnp.float32), weight_last.astype(jnp.float32)).astype(jnp.bfloat16)
    refined_complex = lax.complex(refined[:, :, 0].astype(jnp.float32), refined[:, :, 1].astype(jnp.float32))
    spectra = jnp.fft.fftn(to_complex(coil_maps) * refined_complex[None], axes=(2, 3), norm='ortho')
    model_term = jnp.concatenate([jnp.real(spectra), jnp.imag(spectra)], axis=-1)
    sampled = sample_mask.astype(jnp.float32)
    sampled = jnp.concatenate([sampled, sampled], axis=1)
    current = kspace.astype(jnp.float32)
    updated = (current - step_size[0] * sampled * (current - measured.astype(jnp.float32)) - model_term).astype(jnp.bfloat16)
    adjoint = coil_adjoint(cotangent, coil_maps)
    grad_out = (-adjoint).astype(jnp.bfloat16)
    back_middle, grad_last = pull_back(act_middle, weight_last, grad_out)
    grad_pre_middle = (back_middle * silu_grad(pre_middle)).astype(jnp.bfloat16)
    back_first, grad_middle = pull_back(act_first, weight_middle, grad_pre_middle)
    grad_pre_first = (back_first * silu_grad(pre_first)).astype(jnp.bfloat16)
    _, grad_first = pull_back(layer_zero, weight_first, grad_pre_first)
    return (updated, grad_first, grad_middle, grad_last)
```

```python
import functools
import math

import jax
import jax.numpy as jnp
import numpy as np
from jax import lax
from jax.experimental import pallas as pl
from jax.experimental.pallas import tpu as pltpu
from jax.sharding import PartitionSpec as P


def with_halo(block, sides, width):
    for axis, dim in sides:
        count = lax.axis_size(axis)
        forward = [(i, i + 1) for i in range(count - 1)]
        backward = [(target, source) for source, target in forward]
        low = lax.ppermute(
            lax.slice_in_dim(block, block.shape[dim] - width, None, axis=dim), axis, forward
        )
        high = lax.ppermute(lax.slice_in_dim(block, 0, width, axis=dim), axis, backward)
        block = jnp.concatenate([low, block, high], axis=dim)
    return block


def dft_parts(length):
    position = lax.iota(jnp.int32, length)
    product = position[:, None] * position[None, :] % length
    angles = product.astype(jnp.float32) * (2.0 * math.pi / length)
    factor = 1.0 / math.sqrt(length)
    return (jnp.cos(angles) * factor, jnp.sin(angles) * factor)


def plane_table(length, orient):
    cos_part, sin_part = dft_parts(length)
    upper_rows = jnp.concatenate([cos_part, orient * sin_part], axis=1)
    lower_rows = jnp.concatenate([-orient * sin_part, cos_part], axis=1)
    return jnp.concatenate([upper_rows, lower_rows], axis=0)


def along_y(values, table):
    return jnp.einsum(
        "cxzk,kw->cxzw",
        values,
        table,
        precision=lax.Precision.HIGH,
        preferred_element_type=jnp.float32,
    )


def along_z(values, orient):
    length = values.shape[2]
    half_len = values.shape[3] // 2
    cos_part, sin_part = dft_parts(length)
    stacked = jnp.concatenate([cos_part, sin_part], axis=0)
    mixture = jnp.einsum(
        "wz,cxzk->cxwk",
        stacked,
        values,
        precision=lax.Precision.HIGH,
        preferred_element_type=jnp.float32,
    )
    direct = mixture[:, :, :length]
    crossed = mixture[:, :, length:]
    turned = jnp.concatenate(
        [-orient * crossed[..., half_len:], orient * crossed[..., :half_len]], axis=-1
    )
    return direct + turned


def coil_adjoint(lines, coil_maps):
    half_len = lines.shape[3] // 2
    map_values = coil_maps.astype(jnp.float32)
    map_real = map_values[..., :half_len]
    map_imag = map_values[..., half_len:]
    line_real = lines[..., :half_len]
    line_imag = lines[..., half_len:]
    real_sum = jnp.sum(map_real * line_real + map_imag * line_imag, axis=0)
    imag_sum = jnp.sum(map_real * line_imag - map_imag * line_real, axis=0)
    return jnp.stack([real_sum, imag_sum], axis=2)


def coil_expand(image, coil_maps):
    half_len = coil_maps.shape[3] // 2
    map_values = coil_maps.astype(jnp.float32)
    map_real = map_values[..., :half_len]
    map_imag = map_values[..., half_len:]
    image_real = image[:, :, 0].astype(jnp.float32)
    image_imag = image[:, :, 1].astype(jnp.float32)
    out_real = map_real * image_real - map_imag * image_imag
    out_imag = map_real * image_imag + map_imag * image_real
    return jnp.concatenate([out_real, out_imag], axis=-1)


def with_rims(values):
    return with_halo(values, (("slab", 0), (("coil", "half"), 1)), 1)


def columns_of(padded):
    y_count = padded.shape[3]
    widened = jnp.pad(padded, ((0, 0), (0, 0), (0, 0), (1, 1)))
    return jnp.concatenate(
        [widened[..., shift_y : shift_y + y_count] for shift_y in range(3)], axis=2
    )


def conv_apply(columns, matrix):
    x_count = columns.shape[0] - 2
    z_count = columns.shape[1] - 2
    summed = None
    for shift_x in range(3):
        for shift_z in range(3):
            partial_sum = jnp.einsum(
                "ok,xzky->xzoy",
                matrix[shift_x, shift_z],
                columns[shift_x : shift_x + x_count, shift_z : shift_z + z_count],
                preferred_element_type=jnp.float32,
            )
            summed = partial_sum if summed is None else summed + partial_sum
    return summed


def weight_grad(out_grad, columns):
    x_count = out_grad.shape[0]
    z_count = out_grad.shape[1]
    outer_list = []
    for shift_x in range(3):
        inner_list = []
        for shift_z in range(3):
            inner_list.append(
                jnp.einsum(
                    "xzoy,xzky->ok",
                    out_grad,
                    columns[shift_x : shift_x + x_count, shift_z : shift_z + z_count],
                    preferred_element_type=jnp.float32,
                )
            )
        outer_list.append(jnp.stack(inner_list, axis=0))
    return jnp.stack(outer_list, axis=0)


def as_matrix(weight):
    return weight.reshape(3, 3, weight.shape[2], 3 * weight.shape[4])


def flipped(weight):
    turned = jnp.transpose(jnp.flip(weight, (0, 1, 3)), (0, 1, 4, 3, 2))
    return turned.reshape(3, 3, weight.shape[4], 3 * weight.shape[2])


def silu_grad(values):
    sigma = jax.nn.sigmoid(values)
    return sigma * (1.0 + values * (1.0 - sigma))


def shards_small_chunks(
    kspace,
    measured,
    cotangent,
    coil_maps,
    sample_mask,
    step_size,
    weight_first,
    weight_middle,
    weight_last,
):
    half_len = kspace.shape[3] // 2
    inverse_y = plane_table(half_len, 1.0)
    k_moved, g_moved = (
        lax.all_to_all(kspace, "slab", split_axis=1, concat_axis=2, tiled=True),
        lax.all_to_all(cotangent, "slab", split_axis=1, concat_axis=2, tiled=True),
    )
    k_lines = along_y(k_moved.astype(jnp.float32), inverse_y)
    g_lines = along_y(g_moved.astype(jnp.float32), inverse_y)
    image_full = coil_adjoint(along_z(k_lines, 1.0), coil_maps)
    adjoint_full = coil_adjoint(along_z(g_lines, 1.0), coil_maps)
    summed_image, summed_adjoint = lax.psum((image_full, adjoint_full), ("coil", "half"))
    z_count = summed_image.shape[1] // lax.axis_size(("coil", "half"))
    start = lax.axis_index(("coil", "half")) * z_count
    image = lax.dynamic_slice_in_dim(summed_image, start, z_count, 1)
    adjoint = lax.dynamic_slice_in_dim(summed_adjoint, start, z_count, 1)
    layer_zero = image.astype(jnp.bfloat16)
    cols_zero = columns_of(with_rims(layer_zero))
    pre_first = conv_apply(cols_zero, as_matrix(weight_first))
    act_first = jax.nn.silu(pre_first).astype(jnp.bfloat16)
    cols_first = columns_of(with_rims(act_first))
    pre_middle = conv_apply(cols_first, as_matrix(weight_middle))
    act_middle = jax.nn.silu(pre_middle).astype(jnp.bfloat16)
    cols_middle = columns_of(with_rims(act_middle))
    refined = conv_apply(cols_middle, as_matrix(weight_last)).astype(jnp.bfloat16)
    refined_all = lax.all_gather(refined, ("coil", "half"), axis=1, tiled=True)
    spectra_lines = along_z(coil_expand(refined_all, coil_maps), -1.0)
    spectra_slab = lax.all_to_all(
        spectra_lines.astype(jnp.bfloat16), "slab", split_axis=2, concat_axis=1, tiled=True
    ).astype(spectra_lines.dtype)
    model_term = along_y(spectra_slab, plane_table(half_len, -1.0))
    sampled = sample_mask.astype(jnp.float32)
    sampled = jnp.concatenate([sampled, sampled], axis=1)
    current = kspace.astype(jnp.float32)
    updated = (
        current - step_size[0] * sampled * (current - measured.astype(jnp.float32)) - model_term
    ).astype(jnp.bfloat16)
    grad_out = (-adjoint).astype(jnp.bfloat16)
    grad_last = weight_grad(grad_out, cols_middle)
    back_middle = conv_apply(columns_of(with_rims(grad_out)), flipped(weight_last))
    grad_pre_middle = (back_middle * silu_grad(pre_middle)).astype(jnp.bfloat16)
    grad_middle = weight_grad(grad_pre_middle, cols_first)
    back_first = conv_apply(columns_of(with_rims(grad_pre_middle)), flipped(weight_middle))
    grad_pre_first = (back_first * silu_grad(pre_first)).astype(jnp.bfloat16)
    grad_first = weight_grad(grad_pre_first, cols_zero)
    grad_first, grad_middle, grad_last = lax.psum(
        (grad_first, grad_middle, grad_last), ("slab", "coil", "half")
    )
    return (
        updated,
        grad_first.reshape(weight_first.shape),
        grad_middle.reshape(weight_middle.shape),
        grad_last.reshape(weight_last.shape),
    )


GROUP = ("coil", "half", "slab")


def group_sizes():
    return lax.axis_size("slab"), lax.axis_size("half"), lax.axis_size(GROUP)


def my_position():
    slab_count, half_count, _ = group_sizes()
    coil_half = lax.axis_index("coil") * half_count + lax.axis_index("half")
    return coil_half * slab_count + lax.axis_index("slab")


def device_at(position):
    slab_count, half_count, _ = group_sizes()
    coil_half = lax.div(position, slab_count)
    return {
        "slab": lax.rem(position, slab_count),
        "coil": lax.div(coil_half, half_count),
        "half": lax.rem(coil_half, half_count),
    }


def greet(count, me):
    barrier = pltpu.get_barrier_semaphore()
    for step in range(1, count):
        peer = lax.rem(me + step, count)
        pl.semaphore_signal(
            barrier, inc=1, device_id=device_at(peer), device_id_type=pl.DeviceIdType.MESH
        )
    pl.semaphore_wait(barrier, count - 1)


def send_to(src, dst, send_sem, recv_sem, peer):
    return pltpu.make_async_remote_copy(
        src_ref=src,
        dst_ref=dst,
        send_sem=send_sem,
        recv_sem=recv_sem,
        device_id=device_at(peer),
        device_id_type=pl.DeviceIdType.MESH,
    )


def scatter_slots(count, me, pick, src_ref, dst_ref, send_sem, recv_sem):
    copies = []
    for step in range(1, count):
        peer = lax.rem(me + step, count)
        copy = send_to(
            src_ref.at[pick(peer)], dst_ref.at[me], send_sem.at[step], recv_sem.at[step], peer
        )
        copy.start()
        copies.append(copy)
    dst_ref[me] = src_ref[pick(me)]
    for step in range(1, count):
        source = lax.rem(me + count - step, count)
        send_to(
            src_ref.at[pick(source)],
            dst_ref.at[source],
            send_sem.at[step],
            recv_sem.at[step],
            source,
        ).wait_recv()
    for copy in copies:
        copy.wait_send()


def exchange(values, pick, collective_id):
    _, _, count = group_sizes()

    def kernel(src_ref, dst_ref, send_sem, recv_sem):
        me = my_position()
        greet(count, me)
        scatter_slots(count, me, pick, src_ref, dst_ref, send_sem, recv_sem)

    return pl.pallas_call(
        kernel,
        out_shape=jax.ShapeDtypeStruct((count,) + values.shape[1:], values.dtype),
        in_specs=[pl.BlockSpec(memory_space=pltpu.VMEM)],
        out_specs=pl.BlockSpec(memory_space=pltpu.VMEM),
        scratch_shapes=[pltpu.SemaphoreType.DMA((count,)), pltpu.SemaphoreType.DMA((count,))],
        compiler_params=pltpu.CompilerParams(collective_id=collective_id, has_side_effects=True),
    )(values)


def total_of(values, collective_id):
    _, _, count = group_sizes()

    def kernel(src_ref, dst_ref, parts, own, send_sem, recv_sem, send_two, recv_two):
        me = my_position()
        greet(count, me)
        scatter_slots(count, me, lambda peer: peer, src_ref, parts, send_sem, recv_sem)
        own[0] = jnp.sum(parts[...], axis=0)
        scatter_slots(count, me, lambda peer: 0, own, dst_ref, send_two, recv_two)

    semaphores = pltpu.SemaphoreType.DMA((count,))
    return pl.pallas_call(
        kernel,
        out_shape=jax.ShapeDtypeStruct(values.shape, values.dtype),
        in_specs=[pl.BlockSpec(memory_space=pltpu.VMEM)],
        out_specs=pl.BlockSpec(memory_space=pltpu.VMEM),
        scratch_shapes=[
            pltpu.VMEM(values.shape, values.dtype),
            pltpu.VMEM((1,) + values.shape[1:], values.dtype),
            semaphores,
            semaphores,
            semaphores,
            semaphores,
        ],
        compiler_params=pltpu.CompilerParams(collective_id=collective_id, has_side_effects=True),
    )(values)


def dft_constants(length):
    position = np.arange(length)
    angles = (position[:, None] * position[None, :] % length) * (2.0 * math.pi / length)
    factor = 1.0 / math.sqrt(length)
    return np.cos(angles) * factor, np.sin(angles) * factor


def plane_constant(length, orient):
    cos_part, sin_part = dft_constants(length)
    return jnp.asarray(
        np.block([[cos_part, orient * sin_part], [-orient * sin_part, cos_part]]), jnp.bfloat16
    )


def lines_y(values, orient):
    return jnp.einsum(
        "cxzk,kw->cxzw",
        values,
        plane_constant(values.shape[3] // 2, orient),
        preferred_element_type=jnp.float32,
    )


def lines_z(values, orient):
    length = values.shape[2]
    half_len = values.shape[3] // 2
    cos_part, sin_part = dft_constants(length)
    mixture = jnp.einsum(
        "wz,cxzk->cxwk",
        jnp.asarray(np.concatenate([cos_part, sin_part], axis=0), jnp.bfloat16),
        values,
        preferred_element_type=jnp.float32,
    )
    direct = mixture[:, :, :length]
    crossed = mixture[:, :, length:]
    turned = jnp.concatenate(
        [-orient * crossed[..., half_len:], orient * crossed[..., :half_len]], axis=-1
    )
    return direct + turned


def band_of(x_count):
    shift = np.arange(3)[:, None, None]
    source = np.arange(x_count)[None, :, None]
    target = np.arange(x_count)[None, None, :]
    return (source == target + shift - 1).astype(np.float32)


def banded(weight, x_count):
    band = jnp.asarray(band_of(x_count), jnp.bfloat16)
    wide = jnp.einsum("dzoyi,dab->zyaibo", weight, band, preferred_element_type=jnp.bfloat16)
    return wide.reshape(3, 3, x_count * weight.shape[4], x_count * weight.shape[2])


def conv_rows(rows, kernel):
    return lax.conv_general_dilated(
        rows[None],
        kernel,
        (1, 1),
        [(0, 0), (1, 1)],
        dimension_numbers=("NHWC", "HWIO", "NHWC"),
        preferred_element_type=jnp.float32,
    )[0]


def back_rows(rows, kernel):
    return conv_rows(rows, jnp.transpose(jnp.flip(kernel, (0, 1)), (0, 1, 3, 2)))


def grad_rows(out_grad, rows, x_count):
    z_count, y_count, _ = out_grad.shape
    widened = jnp.pad(rows, ((0, 0), (1, 1), (0, 0)))
    taps = []
    for shift_z in range(3):
        for shift_y in range(3):
            taps.append(
                jnp.einsum(
                    "zyi,zyo->io",
                    widened[shift_z : shift_z + z_count, shift_y : shift_y + y_count],
                    out_grad,
                    preferred_element_type=jnp.float32,
                )
            )
    stacked = jnp.stack(taps).reshape(
        3, 3, x_count, rows.shape[2] // x_count, x_count, out_grad.shape[2] // x_count
    )
    pieces = []
    for shift_x in range(3):
        picked = [
            stacked[:, :, target + shift_x - 1, :, target]
            for target in range(x_count)
            if 0 <= target + shift_x - 1 < x_count
        ]
        pieces.append(functools.reduce(jnp.add, picked))
    return jnp.stack(pieces)


def pixel_rows(slots, slab_count):
    count, z_count, width = slots.shape
    half_len = width // 2
    summed = jnp.sum(
        slots.reshape(count // slab_count, slab_count, z_count, width).astype(jnp.float32), axis=0
    )
    summed = summed.astype(jnp.bfloat16).reshape(slab_count, z_count, 2, half_len)
    return jnp.transpose(summed, (1, 3, 0, 2)).reshape(z_count, half_len, slab_count * 2)


def spread(image, rim, z_count, count):
    flat = image.reshape(image.shape[1], -1).astype(jnp.bfloat16)
    padded = jnp.pad(flat, ((rim, rim), (0, 0)))
    return jnp.stack(
        [padded[spot * z_count : spot * z_count + z_count + 2 * rim] for spot in range(count)]
    )


def shards(
    kspace,
    measured,
    cotangent,
    coil_maps,
    sample_mask,
    step_size,
    weight_first,
    weight_middle,
    weight_last,
):
    slab_count, _, count = group_sizes()
    length = coil_maps.shape[2]
    half_len = kspace.shape[3] // 2
    z_count = length // count
    rim = 4
    if coil_maps.shape[1] != 1 or length % count or z_count % 8:
        return shards_small_chunks(
            kspace,
            measured,
            cotangent,
            coil_maps,
            sample_mask,
            step_size,
            weight_first,
            weight_middle,
            weight_last,
        )
    x_count = slab_count

    def image_slots(values):
        moved = lax.all_to_all(values, "slab", split_axis=1, concat_axis=2, tiled=True)
        lines = lines_y(moved, 1.0).astype(jnp.bfloat16)
        partial_image = coil_adjoint(lines_z(lines, 1.0), coil_maps)
        return spread(partial_image, rim, z_count, count)

    kernel_first = banded(weight_first, x_count)
    kernel_middle = banded(weight_middle, x_count)
    kernel_last = banded(weight_last, x_count)
    layer_zero = pixel_rows(exchange(image_slots(kspace), lambda peer: peer, 0), slab_count)

    first_row = my_position() * z_count
    row_ids = first_row - rim + lax.iota(jnp.int32, z_count + 2 * rim)
    inside = ((row_ids >= 0) & (row_ids < length))[:, None, None]

    def trimmed(values, have, want):
        return values[have - want : values.shape[0] - (have - want)]

    pre_first = conv_rows(trimmed(layer_zero, rim, 3), kernel_first)
    act_first = jnp.where(trimmed(inside, rim, 2), jax.nn.silu(pre_first), 0).astype(jnp.bfloat16)
    pre_middle = conv_rows(act_first, kernel_middle)
    act_middle = jnp.where(trimmed(inside, rim, 1), jax.nn.silu(pre_middle), 0).astype(
        jnp.bfloat16
    )
    refined = conv_rows(act_middle, kernel_last).astype(jnp.bfloat16)
    refined = jnp.transpose(refined.reshape(z_count, half_len, x_count, 2), (2, 0, 3, 1))
    refined = refined.reshape(x_count, z_count * 2, half_len)
    refined_all = exchange(refined, lambda peer: lax.rem(peer, slab_count), 1)
    refined_all = refined_all.reshape(1, length, 2, half_len)

    spectra = lines_z(coil_expand(refined_all, coil_maps).astype(jnp.bfloat16), -1.0)
    spectra_slab = lax.all_to_all(
        spectra.astype(jnp.bfloat16), "slab", split_axis=2, concat_axis=1, tiled=True
    )
    model_term = lines_y(spectra_slab, -1.0)
    sampled = sample_mask.astype(jnp.float32)
    sampled = jnp.concatenate([sampled, sampled], axis=1)
    current = kspace.astype(jnp.float32)
    updated = (
        current - step_size[0] * sampled * (current - measured.astype(jnp.float32)) - model_term
    ).astype(jnp.bfloat16)

    grad_out = -pixel_rows(exchange(image_slots(cotangent), lambda peer: peer, 2), slab_count)
    grad_last = grad_rows(trimmed(grad_out, rim, 0), act_middle, x_count)
    back_middle = back_rows(trimmed(grad_out, rim, 2), kernel_last)
    grad_pre_middle = jnp.where(
        trimmed(inside, rim, 1), back_middle * silu_grad(pre_middle), 0
    ).astype(jnp.bfloat16)
    grad_middle = grad_rows(
        trimmed(grad_pre_middle, 1, 0), trimmed(act_first, 2, 1), x_count
    )
    back_first = back_rows(grad_pre_middle, kernel_middle)
    grad_pre_first = (back_first * silu_grad(trimmed(pre_first, 2, 0))).astype(jnp.bfloat16)
    grad_first = grad_rows(grad_pre_first, trimmed(layer_zero, rim, 1), x_count)

    grads = [grad_first, grad_middle, grad_last]
    packed = jnp.concatenate([grad.reshape(-1) for grad in grads])
    unit = count * 8 * 128
    padding = -packed.shape[0] % unit
    slots = jnp.pad(packed, (0, padding)).reshape(count, -1, 128)
    total = total_of(slots, 3).reshape(-1)
    outs = []
    start = 0
    for grad in grads:
        piece = total[start : start + grad.size].reshape(grad.shape)
        outs.append(jnp.transpose(piece, (0, 1, 4, 2, 3)))
        start += grad.size
    return (updated, *outs)


def solution(mesh):
    return jax.shard_map(
        shards,
        mesh=mesh,
        in_specs=(
            P(("grp", "coil", "half"), None, "slab", None),
            P(("grp", "coil", "half"), None, "slab", None),
            P(("grp", "coil", "half"), None, "slab", None),
            P(("grp", "coil", "half"), "slab", None, None),
            P(("grp", "slab"), None),
            P(),
            P(),
            P(),
            P(),
        ),
        out_specs=(
            P(("grp", "coil", "half"), None, "slab", None),
            P("grp", None, None, None, None),
            P("grp", None, None, None, None),
            P("grp", None, None, None, None),
        ),
        check_vma=False,
    )
```

```python
import functools
import math

import jax
import jax.numpy as jnp
import ml_dtypes
import numpy as np
from jax import lax
from jax.experimental import pallas as pl
from jax.experimental.pallas import tpu as pltpu
from jax.sharding import PartitionSpec as P


def with_halo(block, sides, width):
    for axis, dim in sides:
        count = lax.axis_size(axis)
        forward = [(i, i + 1) for i in range(count - 1)]
        backward = [(target, source) for source, target in forward]
        low = lax.ppermute(
            lax.slice_in_dim(block, block.shape[dim] - width, None, axis=dim), axis, forward
        )
        high = lax.ppermute(lax.slice_in_dim(block, 0, width, axis=dim), axis, backward)
        block = jnp.concatenate([low, block, high], axis=dim)
    return block


def dft_parts(length):
    position = lax.iota(jnp.int32, length)
    product = position[:, None] * position[None, :] % length
    angles = product.astype(jnp.float32) * (2.0 * math.pi / length)
    factor = 1.0 / math.sqrt(length)
    return (jnp.cos(angles) * factor, jnp.sin(angles) * factor)


def plane_table(length, orient):
    cos_part, sin_part = dft_parts(length)
    upper_rows = jnp.concatenate([cos_part, orient * sin_part], axis=1)
    lower_rows = jnp.concatenate([-orient * sin_part, cos_part], axis=1)
    return jnp.concatenate([upper_rows, lower_rows], axis=0)


def along_y(values, table):
    return jnp.einsum(
        "cxzk,kw->cxzw",
        values,
        table,
        precision=lax.Precision.HIGH,
        preferred_element_type=jnp.float32,
    )


def along_z(values, orient):
    length = values.shape[2]
    half_len = values.shape[3] // 2
    cos_part, sin_part = dft_parts(length)
    stacked = jnp.concatenate([cos_part, sin_part], axis=0)
    mixture = jnp.einsum(
        "wz,cxzk->cxwk",
        stacked,
        values,
        precision=lax.Precision.HIGH,
        preferred_element_type=jnp.float32,
    )
    direct = mixture[:, :, :length]
    crossed = mixture[:, :, length:]
    turned = jnp.concatenate(
        [-orient * crossed[..., half_len:], orient * crossed[..., :half_len]], axis=-1
    )
    return direct + turned


def coil_adjoint(lines, coil_maps):
    half_len = lines.shape[3] // 2
    map_values = coil_maps.astype(jnp.float32)
    map_real = map_values[..., :half_len]
    map_imag = map_values[..., half_len:]
    line_real = lines[..., :half_len]
    line_imag = lines[..., half_len:]
    real_sum = jnp.sum(map_real * line_real + map_imag * line_imag, axis=0)
    imag_sum = jnp.sum(map_real * line_imag - map_imag * line_real, axis=0)
    return jnp.stack([real_sum, imag_sum], axis=2)


def coil_expand(image, coil_maps):
    half_len = coil_maps.shape[3] // 2
    map_values = coil_maps.astype(jnp.float32)
    map_real = map_values[..., :half_len]
    map_imag = map_values[..., half_len:]
    image_real = image[:, :, 0].astype(jnp.float32)
    image_imag = image[:, :, 1].astype(jnp.float32)
    out_real = map_real * image_real - map_imag * image_imag
    out_imag = map_real * image_imag + map_imag * image_real
    return jnp.concatenate([out_real, out_imag], axis=-1)


def with_rims(values):
    return with_halo(values, (("slab", 0), (("coil", "half"), 1)), 1)


def columns_of(padded):
    y_count = padded.shape[3]
    widened = jnp.pad(padded, ((0, 0), (0, 0), (0, 0), (1, 1)))
    return jnp.concatenate(
        [widened[..., shift_y : shift_y + y_count] for shift_y in range(3)], axis=2
    )


def conv_apply(columns, matrix):
    x_count = columns.shape[0] - 2
    z_count = columns.shape[1] - 2
    summed = None
    for shift_x in range(3):
        for shift_z in range(3):
            partial_sum = jnp.einsum(
                "ok,xzky->xzoy",
                matrix[shift_x, shift_z],
                columns[shift_x : shift_x + x_count, shift_z : shift_z + z_count],
                preferred_element_type=jnp.float32,
            )
            summed = partial_sum if summed is None else summed + partial_sum
    return summed


def weight_grad(out_grad, columns):
    x_count = out_grad.shape[0]
    z_count = out_grad.shape[1]
    outer_list = []
    for shift_x in range(3):
        inner_list = []
        for shift_z in range(3):
            inner_list.append(
                jnp.einsum(
                    "xzoy,xzky->ok",
                    out_grad,
                    columns[shift_x : shift_x + x_count, shift_z : shift_z + z_count],
                    preferred_element_type=jnp.float32,
                )
            )
        outer_list.append(jnp.stack(inner_list, axis=0))
    return jnp.stack(outer_list, axis=0)


def as_matrix(weight):
    return weight.reshape(3, 3, weight.shape[2], 3 * weight.shape[4])


def flipped(weight):
    turned = jnp.transpose(jnp.flip(weight, (0, 1, 3)), (0, 1, 4, 3, 2))
    return turned.reshape(3, 3, weight.shape[4], 3 * weight.shape[2])


def silu_grad(values):
    sigma = jax.nn.sigmoid(values)
    return sigma * (1.0 + values * (1.0 - sigma))


def shards_small_chunks(
    kspace,
    measured,
    cotangent,
    coil_maps,
    sample_mask,
    step_size,
    weight_first,
    weight_middle,
    weight_last,
):
    half_len = kspace.shape[3] // 2
    inverse_y = plane_table(half_len, 1.0)
    k_moved, g_moved = (
        lax.all_to_all(kspace, "slab", split_axis=1, concat_axis=2, tiled=True),
        lax.all_to_all(cotangent, "slab", split_axis=1, concat_axis=2, tiled=True),
    )
    k_lines = along_y(k_moved.astype(jnp.float32), inverse_y)
    g_lines = along_y(g_moved.astype(jnp.float32), inverse_y)
    image_full = coil_adjoint(along_z(k_lines, 1.0), coil_maps)
    adjoint_full = coil_adjoint(along_z(g_lines, 1.0), coil_maps)
    summed_image, summed_adjoint = lax.psum((image_full, adjoint_full), ("coil", "half"))
    z_count = summed_image.shape[1] // lax.axis_size(("coil", "half"))
    start = lax.axis_index(("coil", "half")) * z_count
    image = lax.dynamic_slice_in_dim(summed_image, start, z_count, 1)
    adjoint = lax.dynamic_slice_in_dim(summed_adjoint, start, z_count, 1)
    layer_zero = image.astype(jnp.bfloat16)
    cols_zero = columns_of(with_rims(layer_zero))
    pre_first = conv_apply(cols_zero, as_matrix(weight_first))
    act_first = jax.nn.silu(pre_first).astype(jnp.bfloat16)
    cols_first = columns_of(with_rims(act_first))
    pre_middle = conv_apply(cols_first, as_matrix(weight_middle))
    act_middle = jax.nn.silu(pre_middle).astype(jnp.bfloat16)
    cols_middle = columns_of(with_rims(act_middle))
    refined = conv_apply(cols_middle, as_matrix(weight_last)).astype(jnp.bfloat16)
    refined_all = lax.all_gather(refined, ("coil", "half"), axis=1, tiled=True)
    spectra_lines = along_z(coil_expand(refined_all, coil_maps), -1.0)
    spectra_slab = lax.all_to_all(
        spectra_lines.astype(jnp.bfloat16), "slab", split_axis=2, concat_axis=1, tiled=True
    ).astype(spectra_lines.dtype)
    model_term = along_y(spectra_slab, plane_table(half_len, -1.0))
    sampled = sample_mask.astype(jnp.float32)
    sampled = jnp.concatenate([sampled, sampled], axis=1)
    current = kspace.astype(jnp.float32)
    updated = (
        current - step_size[0] * sampled * (current - measured.astype(jnp.float32)) - model_term
    ).astype(jnp.bfloat16)
    grad_out = (-adjoint).astype(jnp.bfloat16)
    grad_last = weight_grad(grad_out, cols_middle)
    back_middle = conv_apply(columns_of(with_rims(grad_out)), flipped(weight_last))
    grad_pre_middle = (back_middle * silu_grad(pre_middle)).astype(jnp.bfloat16)
    grad_middle = weight_grad(grad_pre_middle, cols_first)
    back_first = conv_apply(columns_of(with_rims(grad_pre_middle)), flipped(weight_middle))
    grad_pre_first = (back_first * silu_grad(pre_first)).astype(jnp.bfloat16)
    grad_first = weight_grad(grad_pre_first, cols_zero)
    grad_first, grad_middle, grad_last = lax.psum(
        (grad_first, grad_middle, grad_last), ("slab", "coil", "half")
    )
    return (
        updated,
        grad_first.reshape(weight_first.shape),
        grad_middle.reshape(weight_middle.shape),
        grad_last.reshape(weight_last.shape),
    )


GROUP = ("coil", "half", "slab")


def group_sizes():
    return lax.axis_size("slab"), lax.axis_size("half"), lax.axis_size(GROUP)


def my_position():
    slab_count, half_count, _ = group_sizes()
    coil_half = lax.axis_index("coil") * half_count + lax.axis_index("half")
    return coil_half * slab_count + lax.axis_index("slab")


def device_at(position):
    slab_count, half_count, _ = group_sizes()
    coil_half = lax.div(position, slab_count)
    return {
        "slab": lax.rem(position, slab_count),
        "coil": lax.div(coil_half, half_count),
        "half": lax.rem(coil_half, half_count),
    }


def greet(count, me):
    barrier = pltpu.get_barrier_semaphore()
    for step in range(1, count):
        peer = lax.rem(me + step, count)
        pl.semaphore_signal(
            barrier, inc=1, device_id=device_at(peer), device_id_type=pl.DeviceIdType.MESH
        )
    pl.semaphore_wait(barrier, count - 1)


def send_to(src, dst, send_sem, recv_sem, peer):
    return pltpu.make_async_remote_copy(
        src_ref=src,
        dst_ref=dst,
        send_sem=send_sem,
        recv_sem=recv_sem,
        device_id=device_at(peer),
        device_id_type=pl.DeviceIdType.MESH,
    )


def scatter_slots(count, me, pick, src_ref, dst_ref, send_sem, recv_sem):
    copies = []
    for step in range(1, count):
        peer = lax.rem(me + step, count)
        copy = send_to(
            src_ref.at[pick(peer)], dst_ref.at[me], send_sem.at[step], recv_sem.at[step], peer
        )
        copy.start()
        copies.append(copy)
    dst_ref[me] = src_ref[pick(me)]
    for step in range(1, count):
        source = lax.rem(me + count - step, count)
        send_to(
            src_ref.at[pick(source)],
            dst_ref.at[source],
            send_sem.at[step],
            recv_sem.at[step],
            source,
        ).wait_recv()
    for copy in copies:
        copy.wait_send()


def exchange(values, pick, collective_id):
    _, _, count = group_sizes()

    def kernel(src_ref, dst_ref, send_sem, recv_sem):
        me = my_position()
        greet(count, me)
        scatter_slots(count, me, pick, src_ref, dst_ref, send_sem, recv_sem)

    return pl.pallas_call(
        kernel,
        out_shape=jax.ShapeDtypeStruct((count,) + values.shape[1:], values.dtype),
        in_specs=[pl.BlockSpec(memory_space=pltpu.VMEM)],
        out_specs=pl.BlockSpec(memory_space=pltpu.VMEM),
        scratch_shapes=[pltpu.SemaphoreType.DMA((count,)), pltpu.SemaphoreType.DMA((count,))],
        compiler_params=pltpu.CompilerParams(collective_id=collective_id, has_side_effects=True),
    )(values)


def total_of(values, collective_id):
    _, _, count = group_sizes()

    def kernel(src_ref, dst_ref, parts, own, send_sem, recv_sem, send_two, recv_two):
        me = my_position()
        greet(count, me)
        scatter_slots(count, me, lambda peer: peer, src_ref, parts, send_sem, recv_sem)
        own[0] = jnp.sum(parts[...], axis=0)
        scatter_slots(count, me, lambda peer: 0, own, dst_ref, send_two, recv_two)

    semaphores = pltpu.SemaphoreType.DMA((count,))
    return pl.pallas_call(
        kernel,
        out_shape=jax.ShapeDtypeStruct(values.shape, values.dtype),
        in_specs=[pl.BlockSpec(memory_space=pltpu.VMEM)],
        out_specs=pl.BlockSpec(memory_space=pltpu.VMEM),
        scratch_shapes=[
            pltpu.VMEM(values.shape, values.dtype),
            pltpu.VMEM((1,) + values.shape[1:], values.dtype),
            semaphores,
            semaphores,
            semaphores,
            semaphores,
        ],
        compiler_params=pltpu.CompilerParams(collective_id=collective_id, has_side_effects=True),
    )(values)


def dft_constants(length):
    position = np.arange(length)
    angles = (position[:, None] * position[None, :] % length) * (2.0 * math.pi / length)
    factor = 1.0 / math.sqrt(length)
    return np.cos(angles) * factor, np.sin(angles) * factor


def plane_constant(length, orient):
    cos_part, sin_part = dft_constants(length)
    return jnp.asarray(
        np.block([[cos_part, orient * sin_part], [-orient * sin_part, cos_part]]), jnp.bfloat16
    )


def lines_y(values, orient):
    return jnp.einsum(
        "cxzk,kw->cxzw",
        values,
        plane_constant(values.shape[3] // 2, orient),
        preferred_element_type=jnp.float32,
    )


def lines_z(values, orient):
    length = values.shape[2]
    half_len = values.shape[3] // 2
    cos_part, sin_part = dft_constants(length)
    mixture = jnp.einsum(
        "wz,cxzk->cxwk",
        jnp.asarray(np.concatenate([cos_part, sin_part], axis=0), jnp.bfloat16),
        values,
        preferred_element_type=jnp.float32,
    )
    direct = mixture[:, :, :length]
    crossed = mixture[:, :, length:]
    turned = jnp.concatenate(
        [-orient * crossed[..., half_len:], orient * crossed[..., :half_len]], axis=-1
    )
    return direct + turned


def band_of(x_count):
    shift = np.arange(3)[:, None, None]
    source = np.arange(x_count)[None, :, None]
    target = np.arange(x_count)[None, None, :]
    return (source == target + shift - 1).astype(np.float32)


def banded(weight, x_count):
    band = jnp.asarray(band_of(x_count), jnp.bfloat16)
    wide = jnp.einsum("dzoyi,dab->zyaibo", weight, band, preferred_element_type=jnp.bfloat16)
    return wide.reshape(3, 3, x_count * weight.shape[4], x_count * weight.shape[2])


def conv_rows(rows, kernel):
    return lax.conv_general_dilated(
        rows[None],
        kernel,
        (1, 1),
        [(0, 0), (1, 1)],
        dimension_numbers=("NHWC", "HWIO", "NHWC"),
        preferred_element_type=jnp.float32,
    )[0]


def back_rows(rows, kernel):
    return conv_rows(rows, jnp.transpose(jnp.flip(kernel, (0, 1)), (0, 1, 3, 2)))


def grad_rows(out_grad, rows, x_count):
    z_count, y_count, _ = out_grad.shape
    widened = jnp.pad(rows, ((0, 0), (1, 1), (0, 0)))
    taps = []
    for shift_z in range(3):
        for shift_y in range(3):
            taps.append(
                jnp.einsum(
                    "zyi,zyo->io",
                    widened[shift_z : shift_z + z_count, shift_y : shift_y + y_count],
                    out_grad,
                    preferred_element_type=jnp.float32,
                )
            )
    stacked = jnp.stack(taps).reshape(
        3, 3, x_count, rows.shape[2] // x_count, x_count, out_grad.shape[2] // x_count
    )
    pieces = []
    for shift_x in range(3):
        picked = [
            stacked[:, :, target + shift_x - 1, :, target]
            for target in range(x_count)
            if 0 <= target + shift_x - 1 < x_count
        ]
        pieces.append(functools.reduce(jnp.add, picked))
    return jnp.stack(pieces)


def halves_padded(values, wide):
    half_len = values.shape[-1] // 2
    edge = [(0, 0)] * (values.ndim - 1) + [(0, wide - half_len)]
    return jnp.concatenate(
        [jnp.pad(values[..., :half_len], edge), jnp.pad(values[..., half_len:], edge)], axis=-1
    )


def two_parts(table):
    high = table.astype(ml_dtypes.bfloat16)
    low = (table - high.astype(np.float64)).astype(ml_dtypes.bfloat16)
    return jnp.asarray(high), jnp.asarray(low)


def rounded_parts(values):
    high = values.astype(jnp.bfloat16)
    return high, (values - high.astype(jnp.float32)).astype(jnp.bfloat16)


def dot(left, right):
    return jnp.dot(left, right, preferred_element_type=jnp.float32)


def images(kspace, cotangent, coil_maps, rim, collective_id):
    slab_count, _, count = group_sizes()
    coil_count, x_count, slab_rows, width = kspace.shape
    length = slab_count * slab_rows
    half_len = width // 2
    wide = -(-half_len // 128) * 128
    z_count = length // count
    window = z_count + 2 * rim
    tall = length + 2 * rim

    cos_y, sin_y = dft_constants(half_len)
    table_y = np.zeros((width, 2 * wide))
    table_y[:half_len, :half_len] = cos_y
    table_y[:half_len, wide : wide + half_len] = sin_y
    table_y[half_len:, :half_len] = -sin_y
    table_y[half_len:, wide : wide + half_len] = cos_y
    cos_z, sin_z = dft_constants(length)
    table_z = np.zeros((2 * tall, length))
    table_z[rim : rim + length] = cos_z
    table_z[tall + rim : tall + rim + length] = sin_z
    maps = halves_padded(coil_maps[:, 0], wide)
    maps = jnp.pad(maps, ((0, 0), (rim, rim), (0, 0)))

    def kernel(
        k_ref, g_ref, maps_ref, yh_ref, yl_ref, zh_ref, zl_ref, image_ref, adjoint_ref,
        moved, lines, total, slots, parts, send_one, recv_one, send_two, recv_two,
    ):
        me = my_position()
        slab = lax.axis_index("slab")
        greet(count, me)

        def moving(which, step, source_ref, sending):
            offset = step if sending else slab_count - step
            peer = lax.rem(slab + offset, slab_count)
            return pltpu.make_async_remote_copy(
                src_ref=source_ref.at[:, peer],
                dst_ref=moved.at[which, slab if sending else peer],
                send_sem=send_one.at[which, step],
                recv_sem=recv_one.at[which, step],
                device_id={"slab": peer},
                device_id_type=pl.DeviceIdType.MESH,
            )

        def spreading(which, step, sending):
            peer = lax.rem(me + (step if sending else count - step), count)
            return send_to(
                slots.at[which, peer],
                parts.at[which, me if sending else peer],
                send_two.at[which, step],
                recv_two.at[which, step],
                peer,
            )

        sources = (k_ref, g_ref)
        for which in range(2):
            for step in range(1, slab_count):
                moving(which, step, sources[which], True).start()
        for which in range(2):
            moved[which, slab] = sources[which][:, slab]
        for which in range(2):
            for step in range(1, slab_count):
                moving(which, step, sources[which], False).wait_recv()
            for block in range(slab_count):
                rows = moved[which, block].reshape(coil_count * slab_rows, width)
                product = dot(rows, yh_ref[...]) + dot(rows, yl_ref[...])
                lines[:, block * slab_rows : (block + 1) * slab_rows] = product.reshape(
                    coil_count, slab_rows, 2 * wide
                )

            @pl.loop(0, coil_count)
            def _(coil):
                high, low = rounded_parts(lines[coil])
                mixture = dot(zh_ref[...], high) + dot(zh_ref[...], low) + dot(zl_ref[...], high)
                line_real = mixture[:tall, :wide] - mixture[tall:, wide:]
                line_imag = mixture[:tall, wide:] + mixture[tall:, :wide]
                coil_map = maps_ref[coil].astype(jnp.float32)
                map_real, map_imag = coil_map[:, :wide], coil_map[:, wide:]
                real_part = map_real * line_real + map_imag * line_imag
                imag_part = map_real * line_imag - map_imag * line_real
                fresh = jnp.concatenate([real_part, imag_part], axis=1)
                total[...] = jnp.where(coil == 0, fresh, total[...] + fresh)

            for spot in range(count):
                slots[which, spot] = total[spot * z_count : spot * z_count + window].astype(
                    jnp.bfloat16
                )
            for step in range(1, count):
                spreading(which, step, True).start()
            parts[which, me] = slots[which, me]
        outs = (image_ref, adjoint_ref)
        for which in range(2):
            for step in range(1, count):
                spreading(which, step, False).wait_recv()
            for spot in range(slab_count):
                summed = parts[which, spot].astype(jnp.float32)
                for other in range(spot + slab_count, count, slab_count):
                    summed = summed + parts[which, other].astype(jnp.float32)
                outs[which][spot] = summed.astype(jnp.bfloat16)
        for which in range(2):
            for step in range(1, slab_count):
                moving(which, step, sources[which], True).wait_send()
            for step in range(1, count):
                spreading(which, step, True).wait_send()

    shape = jax.ShapeDtypeStruct((slab_count, window, 2 * wide), jnp.bfloat16)
    whole = pl.BlockSpec(memory_space=pltpu.VMEM)
    return pl.pallas_call(
        kernel,
        out_shape=(shape, shape),
        in_specs=[whole] * 7,
        out_specs=(whole, whole),
        scratch_shapes=[
            pltpu.VMEM((2, slab_count, coil_count, slab_rows, width), jnp.bfloat16),
            pltpu.VMEM((coil_count, length, 2 * wide), jnp.float32),
            pltpu.VMEM((tall, 2 * wide), jnp.float32),
            pltpu.VMEM((2, count, window, 2 * wide), jnp.bfloat16),
            pltpu.VMEM((2, count, window, 2 * wide), jnp.bfloat16),
            pltpu.SemaphoreType.DMA((2, slab_count)),
            pltpu.SemaphoreType.DMA((2, slab_count)),
            pltpu.SemaphoreType.DMA((2, count)),
            pltpu.SemaphoreType.DMA((2, count)),
        ],
        compiler_params=pltpu.CompilerParams(
            collective_id=collective_id, has_side_effects=True, vmem_limit_bytes=48 * 2**20
        ),
    )(kspace, cotangent, maps, *two_parts(table_y), *two_parts(table_z))


def pixel_rows(image, half_len):
    slab_count, z_count, width = image.shape
    split = image.reshape(slab_count, z_count, 2, width // 2)[..., :half_len]
    return jnp.transpose(split, (1, 3, 0, 2)).reshape(z_count, half_len, slab_count * 2)


def shards(
    kspace,
    measured,
    cotangent,
    coil_maps,
    sample_mask,
    step_size,
    weight_first,
    weight_middle,
    weight_last,
):
    slab_count, _, count = group_sizes()
    length = coil_maps.shape[2]
    half_len = kspace.shape[3] // 2
    z_count = length // count
    rim = 4
    if coil_maps.shape[1] != 1 or length % count or z_count % 8:
        return shards_small_chunks(
            kspace,
            measured,
            cotangent,
            coil_maps,
            sample_mask,
            step_size,
            weight_first,
            weight_middle,
            weight_last,
        )
    x_count = slab_count

    image, adjoint = images(kspace, cotangent, coil_maps, rim, 0)
    kernel_first = banded(weight_first, x_count)
    kernel_middle = banded(weight_middle, x_count)
    kernel_last = banded(weight_last, x_count)
    layer_zero = pixel_rows(image, half_len)

    first_row = my_position() * z_count
    row_ids = first_row - rim + lax.iota(jnp.int32, z_count + 2 * rim)
    inside = ((row_ids >= 0) & (row_ids < length))[:, None, None]

    def trimmed(values, have, want):
        return values[have - want : values.shape[0] - (have - want)]

    pre_first = conv_rows(trimmed(layer_zero, rim, 3), kernel_first)
    act_first = jnp.where(trimmed(inside, rim, 2), jax.nn.silu(pre_first), 0).astype(jnp.bfloat16)
    pre_middle = conv_rows(act_first, kernel_middle)
    act_middle = jnp.where(trimmed(inside, rim, 1), jax.nn.silu(pre_middle), 0).astype(
        jnp.bfloat16
    )
    refined = conv_rows(act_middle, kernel_last).astype(jnp.bfloat16)
    refined = jnp.transpose(refined.reshape(z_count, half_len, x_count, 2), (2, 0, 3, 1))
    refined = refined.reshape(x_count, z_count * 2, half_len)
    refined_all = exchange(refined, lambda peer: lax.rem(peer, slab_count), 1)
    refined_all = refined_all.reshape(1, length, 2, half_len)

    spectra = lines_z(coil_expand(refined_all, coil_maps).astype(jnp.bfloat16), -1.0)
    spectra_slab = lax.all_to_all(
        spectra.astype(jnp.bfloat16), "slab", split_axis=2, concat_axis=1, tiled=True
    )
    model_term = lines_y(spectra_slab, -1.0)
    sampled = sample_mask.astype(jnp.float32)
    sampled = jnp.concatenate([sampled, sampled], axis=1)
    current = kspace.astype(jnp.float32)
    updated = (
        current - step_size[0] * sampled * (current - measured.astype(jnp.float32)) - model_term
    ).astype(jnp.bfloat16)

    grad_out = -pixel_rows(adjoint, half_len)
    grad_last = grad_rows(trimmed(grad_out, rim, 0), act_middle, x_count)
    back_middle = back_rows(trimmed(grad_out, rim, 2), kernel_last)
    grad_pre_middle = jnp.where(
        trimmed(inside, rim, 1), back_middle * silu_grad(pre_middle), 0
    ).astype(jnp.bfloat16)
    grad_middle = grad_rows(
        trimmed(grad_pre_middle, 1, 0), trimmed(act_first, 2, 1), x_count
    )
    back_first = back_rows(grad_pre_middle, kernel_middle)
    grad_pre_first = (back_first * silu_grad(trimmed(pre_first, 2, 0))).astype(jnp.bfloat16)
    grad_first = grad_rows(grad_pre_first, trimmed(layer_zero, rim, 1), x_count)

    grads = [grad_first, grad_middle, grad_last]
    packed = jnp.concatenate([grad.reshape(-1) for grad in grads])
    unit = count * 8 * 128
    padding = -packed.shape[0] % unit
    slots = jnp.pad(packed, (0, padding)).reshape(count, -1, 128)
    total = total_of(slots, 3).reshape(-1)
    outs = []
    start = 0
    for grad in grads:
        piece = total[start : start + grad.size].reshape(grad.shape)
        outs.append(jnp.transpose(piece, (0, 1, 4, 2, 3)))
        start += grad.size
    return (updated, *outs)


def solution(mesh):
    return jax.shard_map(
        shards,
        mesh=mesh,
        in_specs=(
            P(("grp", "coil", "half"), None, "slab", None),
            P(("grp", "coil", "half"), None, "slab", None),
            P(("grp", "coil", "half"), None, "slab", None),
            P(("grp", "coil", "half"), "slab", None, None),
            P(("grp", "slab"), None),
            P(),
            P(),
            P(),
            P(),
        ),
        out_specs=(
            P(("grp", "coil", "half"), None, "slab", None),
            P("grp", None, None, None, None),
            P("grp", None, None, None, None),
            P("grp", None, None, None, None),
        ),
        check_vma=False,
    )
```

```python
import functools
import math

import jax
import jax.numpy as jnp
import ml_dtypes
import numpy as np
from jax import lax
from jax.experimental import pallas as pl
from jax.experimental.pallas import tpu as pltpu
from jax.sharding import PartitionSpec as P


def with_halo(block, sides, width):
    for axis, dim in sides:
        count = lax.axis_size(axis)
        forward = [(i, i + 1) for i in range(count - 1)]
        backward = [(target, source) for source, target in forward]
        low = lax.ppermute(
            lax.slice_in_dim(block, block.shape[dim] - width, None, axis=dim), axis, forward
        )
        high = lax.ppermute(lax.slice_in_dim(block, 0, width, axis=dim), axis, backward)
        block = jnp.concatenate([low, block, high], axis=dim)
    return block


def dft_parts(length):
    position = lax.iota(jnp.int32, length)
    product = position[:, None] * position[None, :] % length
    angles = product.astype(jnp.float32) * (2.0 * math.pi / length)
    factor = 1.0 / math.sqrt(length)
    return (jnp.cos(angles) * factor, jnp.sin(angles) * factor)


def plane_table(length, orient):
    cos_part, sin_part = dft_parts(length)
    upper_rows = jnp.concatenate([cos_part, orient * sin_part], axis=1)
    lower_rows = jnp.concatenate([-orient * sin_part, cos_part], axis=1)
    return jnp.concatenate([upper_rows, lower_rows], axis=0)


def along_y(values, table):
    return jnp.einsum(
        "cxzk,kw->cxzw",
        values,
        table,
        precision=lax.Precision.HIGH,
        preferred_element_type=jnp.float32,
    )


def along_z(values, orient):
    length = values.shape[2]
    half_len = values.shape[3] // 2
    cos_part, sin_part = dft_parts(length)
    stacked = jnp.concatenate([cos_part, sin_part], axis=0)
    mixture = jnp.einsum(
        "wz,cxzk->cxwk",
        stacked,
        values,
        precision=lax.Precision.HIGH,
        preferred_element_type=jnp.float32,
    )
    direct = mixture[:, :, :length]
    crossed = mixture[:, :, length:]
    turned = jnp.concatenate(
        [-orient * crossed[..., half_len:], orient * crossed[..., :half_len]], axis=-1
    )
    return direct + turned


def coil_adjoint(lines, coil_maps):
    half_len = lines.shape[3] // 2
    map_values = coil_maps.astype(jnp.float32)
    map_real = map_values[..., :half_len]
    map_imag = map_values[..., half_len:]
    line_real = lines[..., :half_len]
    line_imag = lines[..., half_len:]
    real_sum = jnp.sum(map_real * line_real + map_imag * line_imag, axis=0)
    imag_sum = jnp.sum(map_real * line_imag - map_imag * line_real, axis=0)
    return jnp.stack([real_sum, imag_sum], axis=2)


def coil_expand(image, coil_maps):
    half_len = coil_maps.shape[3] // 2
    map_values = coil_maps.astype(jnp.float32)
    map_real = map_values[..., :half_len]
    map_imag = map_values[..., half_len:]
    image_real = image[:, :, 0].astype(jnp.float32)
    image_imag = image[:, :, 1].astype(jnp.float32)
    out_real = map_real * image_real - map_imag * image_imag
    out_imag = map_real * image_imag + map_imag * image_real
    return jnp.concatenate([out_real, out_imag], axis=-1)


def with_rims(values):
    return with_halo(values, (("slab", 0), (("coil", "half"), 1)), 1)


def columns_of(padded):
    y_count = padded.shape[3]
    widened = jnp.pad(padded, ((0, 0), (0, 0), (0, 0), (1, 1)))
    return jnp.concatenate(
        [widened[..., shift_y : shift_y + y_count] for shift_y in range(3)], axis=2
    )


def conv_apply(columns, matrix):
    x_count = columns.shape[0] - 2
    z_count = columns.shape[1] - 2
    summed = None
    for shift_x in range(3):
        for shift_z in range(3):
            partial_sum = jnp.einsum(
                "ok,xzky->xzoy",
                matrix[shift_x, shift_z],
                columns[shift_x : shift_x + x_count, shift_z : shift_z + z_count],
                preferred_element_type=jnp.float32,
            )
            summed = partial_sum if summed is None else summed + partial_sum
    return summed


def weight_grad(out_grad, columns):
    x_count = out_grad.shape[0]
    z_count = out_grad.shape[1]
    outer_list = []
    for shift_x in range(3):
        inner_list = []
        for shift_z in range(3):
            inner_list.append(
                jnp.einsum(
                    "xzoy,xzky->ok",
                    out_grad,
                    columns[shift_x : shift_x + x_count, shift_z : shift_z + z_count],
                    preferred_element_type=jnp.float32,
                )
            )
        outer_list.append(jnp.stack(inner_list, axis=0))
    return jnp.stack(outer_list, axis=0)


def as_matrix(weight):
    return weight.reshape(3, 3, weight.shape[2], 3 * weight.shape[4])


def flipped(weight):
    turned = jnp.transpose(jnp.flip(weight, (0, 1, 3)), (0, 1, 4, 3, 2))
    return turned.reshape(3, 3, weight.shape[4], 3 * weight.shape[2])


def silu_grad(values):
    sigma = jax.nn.sigmoid(values)
    return sigma * (1.0 + values * (1.0 - sigma))


def shards_small_chunks(
    kspace,
    measured,
    cotangent,
    coil_maps,
    sample_mask,
    step_size,
    weight_first,
    weight_middle,
    weight_last,
):
    half_len = kspace.shape[3] // 2
    inverse_y = plane_table(half_len, 1.0)
    k_moved, g_moved = (
        lax.all_to_all(kspace, "slab", split_axis=1, concat_axis=2, tiled=True),
        lax.all_to_all(cotangent, "slab", split_axis=1, concat_axis=2, tiled=True),
    )
    k_lines = along_y(k_moved.astype(jnp.float32), inverse_y)
    g_lines = along_y(g_moved.astype(jnp.float32), inverse_y)
    image_full = coil_adjoint(along_z(k_lines, 1.0), coil_maps)
    adjoint_full = coil_adjoint(along_z(g_lines, 1.0), coil_maps)
    summed_image, summed_adjoint = lax.psum((image_full, adjoint_full), ("coil", "half"))
    z_count = summed_image.shape[1] // lax.axis_size(("coil", "half"))
    start = lax.axis_index(("coil", "half")) * z_count
    image = lax.dynamic_slice_in_dim(summed_image, start, z_count, 1)
    adjoint = lax.dynamic_slice_in_dim(summed_adjoint, start, z_count, 1)
    layer_zero = image.astype(jnp.bfloat16)
    cols_zero = columns_of(with_rims(layer_zero))
    pre_first = conv_apply(cols_zero, as_matrix(weight_first))
    act_first = jax.nn.silu(pre_first).astype(jnp.bfloat16)
    cols_first = columns_of(with_rims(act_first))
    pre_middle = conv_apply(cols_first, as_matrix(weight_middle))
    act_middle = jax.nn.silu(pre_middle).astype(jnp.bfloat16)
    cols_middle = columns_of(with_rims(act_middle))
    refined = conv_apply(cols_middle, as_matrix(weight_last)).astype(jnp.bfloat16)
    refined_all = lax.all_gather(refined, ("coil", "half"), axis=1, tiled=True)
    spectra_lines = along_z(coil_expand(refined_all, coil_maps), -1.0)
    spectra_slab = lax.all_to_all(
        spectra_lines.astype(jnp.bfloat16), "slab", split_axis=2, concat_axis=1, tiled=True
    ).astype(spectra_lines.dtype)
    model_term = along_y(spectra_slab, plane_table(half_len, -1.0))
    sampled = sample_mask.astype(jnp.float32)
    sampled = jnp.concatenate([sampled, sampled], axis=1)
    current = kspace.astype(jnp.float32)
    updated = (
        current - step_size[0] * sampled * (current - measured.astype(jnp.float32)) - model_term
    ).astype(jnp.bfloat16)
    grad_out = (-adjoint).astype(jnp.bfloat16)
    grad_last = weight_grad(grad_out, cols_middle)
    back_middle = conv_apply(columns_of(with_rims(grad_out)), flipped(weight_last))
    grad_pre_middle = (back_middle * silu_grad(pre_middle)).astype(jnp.bfloat16)
    grad_middle = weight_grad(grad_pre_middle, cols_first)
    back_first = conv_apply(columns_of(with_rims(grad_pre_middle)), flipped(weight_middle))
    grad_pre_first = (back_first * silu_grad(pre_first)).astype(jnp.bfloat16)
    grad_first = weight_grad(grad_pre_first, cols_zero)
    grad_first, grad_middle, grad_last = lax.psum(
        (grad_first, grad_middle, grad_last), ("slab", "coil", "half")
    )
    return (
        updated,
        grad_first.reshape(weight_first.shape),
        grad_middle.reshape(weight_middle.shape),
        grad_last.reshape(weight_last.shape),
    )


GROUP = ("coil", "half", "slab")


def group_sizes():
    return lax.axis_size("slab"), lax.axis_size("half"), lax.axis_size(GROUP)


def my_position():
    slab_count, half_count, _ = group_sizes()
    coil_half = lax.axis_index("coil") * half_count + lax.axis_index("half")
    return coil_half * slab_count + lax.axis_index("slab")


def device_at(position):
    slab_count, half_count, _ = group_sizes()
    coil_half = lax.div(position, slab_count)
    return {
        "slab": lax.rem(position, slab_count),
        "coil": lax.div(coil_half, half_count),
        "half": lax.rem(coil_half, half_count),
    }


def greet(count, me):
    barrier = pltpu.get_barrier_semaphore()
    for step in range(1, count):
        peer = lax.rem(me + step, count)
        pl.semaphore_signal(
            barrier, inc=1, device_id=device_at(peer), device_id_type=pl.DeviceIdType.MESH
        )
    pl.semaphore_wait(barrier, count - 1)


def send_to(src, dst, send_sem, recv_sem, peer):
    return pltpu.make_async_remote_copy(
        src_ref=src,
        dst_ref=dst,
        send_sem=send_sem,
        recv_sem=recv_sem,
        device_id=device_at(peer),
        device_id_type=pl.DeviceIdType.MESH,
    )


def scatter_slots(count, me, pick, src_ref, dst_ref, send_sem, recv_sem):
    copies = []
    for step in range(1, count):
        peer = lax.rem(me + step, count)
        copy = send_to(
            src_ref.at[pick(peer)], dst_ref.at[me], send_sem.at[step], recv_sem.at[step], peer
        )
        copy.start()
        copies.append(copy)
    dst_ref[me] = src_ref[pick(me)]
    for step in range(1, count):
        source = lax.rem(me + count - step, count)
        send_to(
            src_ref.at[pick(source)],
            dst_ref.at[source],
            send_sem.at[step],
            recv_sem.at[step],
            source,
        ).wait_recv()
    for copy in copies:
        copy.wait_send()


def exchange(values, pick, collective_id):
    _, _, count = group_sizes()

    def kernel(src_ref, dst_ref, send_sem, recv_sem):
        me = my_position()
        greet(count, me)
        scatter_slots(count, me, pick, src_ref, dst_ref, send_sem, recv_sem)

    return pl.pallas_call(
        kernel,
        out_shape=jax.ShapeDtypeStruct((count,) + values.shape[1:], values.dtype),
        in_specs=[pl.BlockSpec(memory_space=pltpu.VMEM)],
        out_specs=pl.BlockSpec(memory_space=pltpu.VMEM),
        scratch_shapes=[pltpu.SemaphoreType.DMA((count,)), pltpu.SemaphoreType.DMA((count,))],
        compiler_params=pltpu.CompilerParams(collective_id=collective_id, has_side_effects=True),
    )(values)


def total_of(values, collective_id):
    _, _, count = group_sizes()

    def kernel(src_ref, dst_ref, parts, own, send_sem, recv_sem, send_two, recv_two):
        me = my_position()
        greet(count, me)
        scatter_slots(count, me, lambda peer: peer, src_ref, parts, send_sem, recv_sem)
        own[0] = jnp.sum(parts[...], axis=0)
        scatter_slots(count, me, lambda peer: 0, own, dst_ref, send_two, recv_two)

    semaphores = pltpu.SemaphoreType.DMA((count,))
    return pl.pallas_call(
        kernel,
        out_shape=jax.ShapeDtypeStruct(values.shape, values.dtype),
        in_specs=[pl.BlockSpec(memory_space=pltpu.VMEM)],
        out_specs=pl.BlockSpec(memory_space=pltpu.VMEM),
        scratch_shapes=[
            pltpu.VMEM(values.shape, values.dtype),
            pltpu.VMEM((1,) + values.shape[1:], values.dtype),
            semaphores,
            semaphores,
            semaphores,
            semaphores,
        ],
        compiler_params=pltpu.CompilerParams(collective_id=collective_id, has_side_effects=True),
    )(values)


def dft_constants(length):
    position = np.arange(length)
    angles = (position[:, None] * position[None, :] % length) * (2.0 * math.pi / length)
    factor = 1.0 / math.sqrt(length)
    return np.cos(angles) * factor, np.sin(angles) * factor


def plane_constant(length, orient):
    cos_part, sin_part = dft_constants(length)
    return jnp.asarray(
        np.block([[cos_part, orient * sin_part], [-orient * sin_part, cos_part]]), jnp.bfloat16
    )


def lines_y(values, orient):
    return jnp.einsum(
        "cxzk,kw->cxzw",
        values,
        plane_constant(values.shape[3] // 2, orient),
        preferred_element_type=jnp.float32,
    )


def lines_z(values, orient):
    length = values.shape[2]
    half_len = values.shape[3] // 2
    cos_part, sin_part = dft_constants(length)
    mixture = jnp.einsum(
        "wz,cxzk->cxwk",
        jnp.asarray(np.concatenate([cos_part, sin_part], axis=0), jnp.bfloat16),
        values,
        preferred_element_type=jnp.float32,
    )
    direct = mixture[:, :, :length]
    crossed = mixture[:, :, length:]
    turned = jnp.concatenate(
        [-orient * crossed[..., half_len:], orient * crossed[..., :half_len]], axis=-1
    )
    return direct + turned


def band_of(x_count):
    shift = np.arange(3)[:, None, None]
    source = np.arange(x_count)[None, :, None]
    target = np.arange(x_count)[None, None, :]
    return (source == target + shift - 1).astype(np.float32)


def banded(weight, x_count):
    band = jnp.asarray(band_of(x_count), jnp.bfloat16)
    wide = jnp.einsum("dzoyi,dab->zyaibo", weight, band, preferred_element_type=jnp.bfloat16)
    return wide.reshape(3, 3, x_count * weight.shape[4], x_count * weight.shape[2])


def halves_padded(values, wide):
    half_len = values.shape[-1] // 2
    edge = [(0, 0)] * (values.ndim - 1) + [(0, wide - half_len)]
    return jnp.concatenate(
        [jnp.pad(values[..., :half_len], edge), jnp.pad(values[..., half_len:], edge)], axis=-1
    )


def two_parts(table):
    high = table.astype(ml_dtypes.bfloat16)
    low = (table - high.astype(np.float64)).astype(ml_dtypes.bfloat16)
    return jnp.asarray(high), jnp.asarray(low)


def rounded_parts(values):
    high = values.astype(jnp.bfloat16)
    return high, (values - high.astype(jnp.float32)).astype(jnp.bfloat16)


def dot(left, right):
    return jnp.dot(left, right, preferred_element_type=jnp.float32)


def images(kspace, cotangent, coil_maps, rim, collective_id):
    slab_count, _, count = group_sizes()
    coil_count, x_count, slab_rows, width = kspace.shape
    length = slab_count * slab_rows
    half_len = width // 2
    wide = -(-half_len // 128) * 128
    z_count = length // count
    window = z_count + 2 * rim
    tall = length + 2 * rim

    cos_y, sin_y = dft_constants(half_len)
    table_y = np.zeros((width, 2 * wide))
    table_y[:half_len, :half_len] = cos_y
    table_y[:half_len, wide : wide + half_len] = sin_y
    table_y[half_len:, :half_len] = -sin_y
    table_y[half_len:, wide : wide + half_len] = cos_y
    cos_z, sin_z = dft_constants(length)
    table_z = np.zeros((2 * tall, length))
    table_z[rim : rim + length] = cos_z
    table_z[tall + rim : tall + rim + length] = sin_z
    maps = halves_padded(coil_maps[:, 0], wide)
    maps = jnp.pad(maps, ((0, 0), (rim, rim), (0, 0)))

    def kernel(
        k_ref, g_ref, maps_ref, yh_ref, yl_ref, zh_ref, zl_ref, image_ref, adjoint_ref,
        moved, lines, total, slots, parts, send_one, recv_one, send_two, recv_two,
    ):
        me = my_position()
        slab = lax.axis_index("slab")
        greet(count, me)

        def moving(which, step, source_ref, sending):
            offset = step if sending else slab_count - step
            peer = lax.rem(slab + offset, slab_count)
            return pltpu.make_async_remote_copy(
                src_ref=source_ref.at[:, peer],
                dst_ref=moved.at[which, slab if sending else peer],
                send_sem=send_one.at[which, step],
                recv_sem=recv_one.at[which, step],
                device_id={"slab": peer},
                device_id_type=pl.DeviceIdType.MESH,
            )

        def spreading(which, step, sending):
            peer = lax.rem(me + (step if sending else count - step), count)
            return send_to(
                slots.at[which, peer],
                parts.at[which, me if sending else peer],
                send_two.at[which, step],
                recv_two.at[which, step],
                peer,
            )

        sources = (k_ref, g_ref)
        for which in range(2):
            for step in range(1, slab_count):
                moving(which, step, sources[which], True).start()
        for which in range(2):
            moved[which, slab] = sources[which][:, slab]
        for which in range(2):
            for step in range(1, slab_count):
                moving(which, step, sources[which], False).wait_recv()
            for block in range(slab_count):
                rows = moved[which, block].reshape(coil_count * slab_rows, width)
                product = dot(rows, yh_ref[...]) + dot(rows, yl_ref[...])
                lines[:, block * slab_rows : (block + 1) * slab_rows] = product.reshape(
                    coil_count, slab_rows, 2 * wide
                )

            @pl.loop(0, coil_count)
            def _(coil):
                high, low = rounded_parts(lines[coil])
                mixture = dot(zh_ref[...], high) + dot(zh_ref[...], low) + dot(zl_ref[...], high)
                line_real = mixture[:tall, :wide] - mixture[tall:, wide:]
                line_imag = mixture[:tall, wide:] + mixture[tall:, :wide]
                coil_map = maps_ref[coil].astype(jnp.float32)
                map_real, map_imag = coil_map[:, :wide], coil_map[:, wide:]
                real_part = map_real * line_real + map_imag * line_imag
                imag_part = map_real * line_imag - map_imag * line_real
                fresh = jnp.concatenate([real_part, imag_part], axis=1)
                total[...] = jnp.where(coil == 0, fresh, total[...] + fresh)

            for spot in range(count):
                slots[which, spot] = total[spot * z_count : spot * z_count + window].astype(
                    jnp.bfloat16
                )
            for step in range(1, count):
                spreading(which, step, True).start()
            parts[which, me] = slots[which, me]
        outs = (image_ref, adjoint_ref)
        for which in range(2):
            for step in range(1, count):
                spreading(which, step, False).wait_recv()
            for spot in range(slab_count):
                summed = parts[which, spot].astype(jnp.float32)
                for other in range(spot + slab_count, count, slab_count):
                    summed = summed + parts[which, other].astype(jnp.float32)
                summed = summed.astype(jnp.bfloat16).astype(jnp.float32)
                outs[which][:, 2 * spot, :] = summed[:, :wide]
                outs[which][:, 2 * spot + 1, :] = summed[:, wide:]
        for which in range(2):
            for step in range(1, slab_count):
                moving(which, step, sources[which], True).wait_send()
            for step in range(1, count):
                spreading(which, step, True).wait_send()

    shape = jax.ShapeDtypeStruct((window, 2 * slab_count, wide), jnp.float32)
    whole = pl.BlockSpec(memory_space=pltpu.VMEM)
    return pl.pallas_call(
        kernel,
        out_shape=(shape, shape),
        in_specs=[whole] * 7,
        out_specs=(whole, whole),
        scratch_shapes=[
            pltpu.VMEM((2, slab_count, coil_count, slab_rows, width), jnp.bfloat16),
            pltpu.VMEM((coil_count, length, 2 * wide), jnp.float32),
            pltpu.VMEM((tall, 2 * wide), jnp.float32),
            pltpu.VMEM((2, count, window, 2 * wide), jnp.bfloat16),
            pltpu.VMEM((2, count, window, 2 * wide), jnp.bfloat16),
            pltpu.SemaphoreType.DMA((2, slab_count)),
            pltpu.SemaphoreType.DMA((2, slab_count)),
            pltpu.SemaphoreType.DMA((2, count)),
            pltpu.SemaphoreType.DMA((2, count)),
        ],
        compiler_params=pltpu.CompilerParams(
            collective_id=collective_id, has_side_effects=True, vmem_limit_bytes=48 * 2**20
        ),
    )(kspace, cotangent, maps, *two_parts(table_y), *two_parts(table_z))


LANES = 128


def tap_rows(kernel):
    edge = [(0, 0), (0, 0), (0, LANES - kernel.shape[2]), (0, LANES - kernel.shape[3])]
    return jnp.pad(kernel, edge).reshape(3, 3 * LANES, LANES)


def back_taps(kernel):
    return jnp.transpose(jnp.flip(kernel, (0, 1)), (0, 1, 3, 2))


def pixels_of(plane, y_count):
    filler = jnp.zeros((LANES - plane.shape[0], plane.shape[1]), plane.dtype)
    return jnp.concatenate([plane, filler], axis=0).T[:y_count]


def fill_taps(taps_ref, row, values):
    y_count = values.shape[0]
    position = lax.broadcasted_iota(jnp.int32, values.shape, 0)
    before = jnp.where(position == 0, 0.0, pltpu.roll(values, 1, 0))
    after = jnp.where(position == y_count - 1, 0.0, pltpu.roll(values, y_count - 1, 0))
    taps_ref[row, :, :LANES] = before.astype(jnp.bfloat16)
    taps_ref[row, :, LANES : 2 * LANES] = values.astype(jnp.bfloat16)
    taps_ref[row, :, 2 * LANES :] = after.astype(jnp.bfloat16)


def conv_row(taps_ref, weight_ref, row):
    summed = dot(taps_ref[row], weight_ref[0])
    for shift_z in range(1, 3):
        summed = summed + dot(taps_ref[row + shift_z], weight_ref[shift_z])
    return summed


def row_inside(row, me, z_count, length):
    place = me * z_count + row
    return jnp.logical_and(place >= 0, place < length)


def forward_layers(image, weights, z_count, length, y_count):
    def kernel(
        image_ref, first_ref, middle_ref, last_ref,
        refined_ref, taps_zero, taps_first, taps_middle, pre_first, pre_middle,
    ):
        me = my_position()

        @pl.loop(0, z_count + 6)
        def _(row):
            fill_taps(taps_zero, row, pixels_of(image_ref[row + 1], y_count))

        @pl.loop(0, z_count + 4)
        def _(row):
            pre = conv_row(taps_zero, first_ref, row)
            pre_first[row] = pre
            act = pre / (1.0 + jnp.exp(-pre))
            fill_taps(
                taps_first, row, jnp.where(row_inside(row - 2, me, z_count, length), act, 0.0)
            )

        @pl.loop(0, z_count + 2)
        def _(row):
            pre = conv_row(taps_first, middle_ref, row)
            pre_middle[row] = pre
            act = pre / (1.0 + jnp.exp(-pre))
            fill_taps(
                taps_middle, row, jnp.where(row_inside(row - 1, me, z_count, length), act, 0.0)
            )

        @pl.loop(0, z_count)
        def _(row):
            refined_ref[row] = conv_row(taps_middle, last_ref, row).T[: refined_ref.shape[1]]

    def taps(extra):
        return jax.ShapeDtypeStruct((z_count + extra, y_count, 3 * LANES), jnp.bfloat16)

    def full(extra):
        return jax.ShapeDtypeStruct((z_count + extra, y_count, LANES), jnp.float32)

    whole = pl.BlockSpec(memory_space=pltpu.VMEM)
    return pl.pallas_call(
        kernel,
        out_shape=(
            jax.ShapeDtypeStruct((z_count, image.shape[1], y_count), jnp.float32),
            taps(6), taps(4), taps(2), full(4), full(2),
        ),
        in_specs=[whole] * 4,
        out_specs=(whole,) * 6,
        compiler_params=pltpu.CompilerParams(vmem_limit_bytes=48 * 2**20),
    )(image, *weights)


def backward_layers(
    adjoint, taps_zero, taps_first, taps_middle, pre_first, pre_middle, weights,
    z_count, length, y_count, x_count, slot_rows,
):
    channels = LANES // x_count
    few = adjoint.shape[1]

    def kernel(
        adjoint_ref, zero_ref, first_ref, middle_ref, pre_first_ref, pre_middle_ref,
        back_middle_ref, back_last_ref, out_ref, out_taps, grad_taps, sums,
    ):
        me = my_position()

        @pl.loop(0, z_count + 4)
        def _(row):
            fill_taps(out_taps, row, -pixels_of(adjoint_ref[row + 2], y_count))

        @pl.loop(0, z_count + 2)
        def _(row):
            grad = conv_row(out_taps, back_last_ref, row) * silu_grad(pre_middle_ref[row])
            fill_taps(
                grad_taps, row, jnp.where(row_inside(row - 1, me, z_count, length), grad, 0.0)
            )

        sums[...] = jnp.zeros_like(sums)

        def gather(which, grad, taps_ref, row):
            for shift_z in range(3):
                sums[which, shift_z] += lax.dot_general(
                    grad,
                    taps_ref[row + shift_z],
                    (((0,), (0,)), ((), ())),
                    preferred_element_type=jnp.float32,
                )

        @pl.loop(0, z_count)
        def _(row):
            grad = conv_row(grad_taps, back_middle_ref, row) * silu_grad(pre_first_ref[row + 2])
            gather(0, grad.astype(jnp.bfloat16), zero_ref, row + 2)
            gather(1, grad_taps[row + 1, :, LANES : 2 * LANES], first_ref, row + 1)
            gather(2, out_taps[row + 2, :, LANES : 2 * LANES], middle_ref, row)

        out_ref[...] = jnp.zeros_like(out_ref)
        group = lax.broadcasted_iota(jnp.int32, (channels, LANES), 1) // channels
        for shift_z in range(3):
            for shift_y in range(3):
                tap = shift_z * 3 + shift_y
                lanes = slice(shift_y * LANES, (shift_y + 1) * LANES)
                square = sums[1, shift_z, :, lanes]
                folded = jnp.zeros((channels, LANES), jnp.float32)
                for shift_x in range(3):
                    picked = jnp.zeros((channels, LANES), jnp.float32)
                    for spot in range(x_count):
                        picked = picked + jnp.where(
                            group == spot + shift_x - 1,
                            square[spot * channels : (spot + 1) * channels],
                            0.0,
                        )
                    turn = LANES // 2
                    while turn >= channels:
                        picked = picked + pltpu.roll(picked, turn, 1)
                        turn //= 2
                    folded = jnp.where(group == shift_x, picked, folded)
                out_ref[tap * channels : (tap + 1) * channels] = folded
                base = 9 * channels + tap * few
                out_ref[base : base + few] = sums[0, shift_z, :, lanes].T[:few]
                base = base + 9 * few
                out_ref[base : base + few] = sums[2, shift_z, :few, lanes]

    whole = pl.BlockSpec(memory_space=pltpu.VMEM)
    return pl.pallas_call(
        kernel,
        out_shape=jax.ShapeDtypeStruct((slot_rows, LANES), jnp.float32),
        in_specs=[whole] * 8,
        out_specs=whole,
        scratch_shapes=[
            pltpu.VMEM((z_count + 4, y_count, 3 * LANES), jnp.bfloat16),
            pltpu.VMEM((z_count + 2, y_count, 3 * LANES), jnp.bfloat16),
            pltpu.VMEM((3, 3, LANES, 3 * LANES), jnp.float32),
        ],
        compiler_params=pltpu.CompilerParams(vmem_limit_bytes=56 * 2**20),
    )(adjoint, taps_zero, taps_first, taps_middle, pre_first, pre_middle, *weights)


def band_sums(pairs, x_count):
    pieces = []
    for shift_x in range(3):
        picked = [
            pairs(target + shift_x - 1, target)
            for target in range(x_count)
            if 0 <= target + shift_x - 1 < x_count
        ]
        pieces.append(functools.reduce(jnp.add, picked))
    return jnp.stack(pieces)


def shards(
    kspace,
    measured,
    cotangent,
    coil_maps,
    sample_mask,
    step_size,
    weight_first,
    weight_middle,
    weight_last,
):
    slab_count, _, count = group_sizes()
    length = coil_maps.shape[2]
    half_len = kspace.shape[3] // 2
    z_count = length // count
    rim = 4
    lanes = slab_count * weight_middle.shape[2]
    if coil_maps.shape[1] != 1 or length % count or z_count % 8 or lanes != LANES or half_len % 16:
        return shards_small_chunks(
            kspace,
            measured,
            cotangent,
            coil_maps,
            sample_mask,
            step_size,
            weight_first,
            weight_middle,
            weight_last,
        )
    x_count = slab_count

    image, adjoint = images(kspace, cotangent, coil_maps, rim, 0)
    kernel_first = banded(weight_first, x_count)
    kernel_middle = banded(weight_middle, x_count)
    kernel_last = banded(weight_last, x_count)
    refined, *kept = forward_layers(
        image,
        (tap_rows(kernel_first), tap_rows(kernel_middle), tap_rows(kernel_last)),
        z_count,
        length,
        half_len,
    )
    refined = refined.astype(jnp.bfloat16).reshape(z_count, x_count, 2, half_len)
    refined = jnp.transpose(refined, (1, 0, 2, 3)).reshape(x_count, z_count * 2, half_len)
    refined_all = exchange(refined, lambda peer: lax.rem(peer, slab_count), 1)
    refined_all = refined_all.reshape(1, length, 2, half_len)

    spectra = lines_z(coil_expand(refined_all, coil_maps).astype(jnp.bfloat16), -1.0)
    spectra_slab = lax.all_to_all(
        spectra.astype(jnp.bfloat16), "slab", split_axis=2, concat_axis=1, tiled=True
    )
    model_term = lines_y(spectra_slab, -1.0)
    sampled = sample_mask.astype(jnp.float32)
    sampled = jnp.concatenate([sampled, sampled], axis=1)
    current = kspace.astype(jnp.float32)
    updated = (
        current - step_size[0] * sampled * (current - measured.astype(jnp.float32)) - model_term
    ).astype(jnp.bfloat16)

    channels = LANES // x_count
    few = 2 * x_count
    used = 9 * (channels + 2 * few)
    slot_rows = -(-used // (8 * count)) * 8 * count
    local = backward_layers(
        adjoint,
        *kept,
        (tap_rows(back_taps(kernel_middle)), tap_rows(back_taps(kernel_last))),
        z_count,
        length,
        half_len,
        x_count,
        slot_rows,
    )
    total = total_of(local.reshape(count, -1, LANES), 3).reshape(slot_rows, LANES)
    wide_rows = 9 * channels
    middle = total[:wide_rows].reshape(3, 3, channels, x_count, channels)[:, :, :, :3]
    first = total[wide_rows : wide_rows + 9 * few].reshape(3, 3, x_count, 2, x_count, channels)
    last = total[wide_rows + 9 * few : used].reshape(3, 3, x_count, 2, x_count, channels)
    grad_middle = jnp.transpose(middle, (3, 0, 2, 1, 4))
    grad_first = band_sums(lambda source, target: first[:, :, source, :, target], x_count)
    grad_last = band_sums(lambda source, target: last[:, :, target, :, source], x_count)
    return (
        updated,
        jnp.transpose(grad_first, (0, 1, 4, 2, 3)),
        grad_middle,
        jnp.transpose(grad_last, (0, 1, 3, 2, 4)),
    )


def solution(mesh):
    return jax.shard_map(
        shards,
        mesh=mesh,
        in_specs=(
            P(("grp", "coil", "half"), None, "slab", None),
            P(("grp", "coil", "half"), None, "slab", None),
            P(("grp", "coil", "half"), None, "slab", None),
            P(("grp", "coil", "half"), "slab", None, None),
            P(("grp", "slab"), None),
            P(),
            P(),
            P(),
            P(),
        ),
        out_specs=(
            P(("grp", "coil", "half"), None, "slab", None),
            P("grp", None, None, None, None),
            P("grp", None, None, None, None),
            P("grp", None, None, None, None),
        ),
        check_vma=False,
    )
```

```python
import functools
import math

import jax
import jax.numpy as jnp
import ml_dtypes
import numpy as np
from jax import lax
from jax.experimental import pallas as pl
from jax.experimental.pallas import tpu as pltpu
from jax.sharding import PartitionSpec as P


def with_halo(block, sides, width):
    for axis, dim in sides:
        count = lax.axis_size(axis)
        forward = [(i, i + 1) for i in range(count - 1)]
        backward = [(target, source) for source, target in forward]
        low = lax.ppermute(
            lax.slice_in_dim(block, block.shape[dim] - width, None, axis=dim), axis, forward
        )
        high = lax.ppermute(lax.slice_in_dim(block, 0, width, axis=dim), axis, backward)
        block = jnp.concatenate([low, block, high], axis=dim)
    return block


def dft_parts(length):
    position = lax.iota(jnp.int32, length)
    product = position[:, None] * position[None, :] % length
    angles = product.astype(jnp.float32) * (2.0 * math.pi / length)
    factor = 1.0 / math.sqrt(length)
    return (jnp.cos(angles) * factor, jnp.sin(angles) * factor)


def plane_table(length, orient):
    cos_part, sin_part = dft_parts(length)
    upper_rows = jnp.concatenate([cos_part, orient * sin_part], axis=1)
    lower_rows = jnp.concatenate([-orient * sin_part, cos_part], axis=1)
    return jnp.concatenate([upper_rows, lower_rows], axis=0)


def along_y(values, table):
    return jnp.einsum(
        "cxzk,kw->cxzw",
        values,
        table,
        precision=lax.Precision.HIGH,
        preferred_element_type=jnp.float32,
    )


def along_z(values, orient):
    length = values.shape[2]
    half_len = values.shape[3] // 2
    cos_part, sin_part = dft_parts(length)
    stacked = jnp.concatenate([cos_part, sin_part], axis=0)
    mixture = jnp.einsum(
        "wz,cxzk->cxwk",
        stacked,
        values,
        precision=lax.Precision.HIGH,
        preferred_element_type=jnp.float32,
    )
    direct = mixture[:, :, :length]
    crossed = mixture[:, :, length:]
    turned = jnp.concatenate(
        [-orient * crossed[..., half_len:], orient * crossed[..., :half_len]], axis=-1
    )
    return direct + turned


def coil_adjoint(lines, coil_maps):
    half_len = lines.shape[3] // 2
    map_values = coil_maps.astype(jnp.float32)
    map_real = map_values[..., :half_len]
    map_imag = map_values[..., half_len:]
    line_real = lines[..., :half_len]
    line_imag = lines[..., half_len:]
    real_sum = jnp.sum(map_real * line_real + map_imag * line_imag, axis=0)
    imag_sum = jnp.sum(map_real * line_imag - map_imag * line_real, axis=0)
    return jnp.stack([real_sum, imag_sum], axis=2)


def coil_expand(image, coil_maps):
    half_len = coil_maps.shape[3] // 2
    map_values = coil_maps.astype(jnp.float32)
    map_real = map_values[..., :half_len]
    map_imag = map_values[..., half_len:]
    image_real = image[:, :, 0].astype(jnp.float32)
    image_imag = image[:, :, 1].astype(jnp.float32)
    out_real = map_real * image_real - map_imag * image_imag
    out_imag = map_real * image_imag + map_imag * image_real
    return jnp.concatenate([out_real, out_imag], axis=-1)


def with_rims(values):
    return with_halo(values, (("slab", 0), (("coil", "half"), 1)), 1)


def columns_of(padded):
    y_count = padded.shape[3]
    widened = jnp.pad(padded, ((0, 0), (0, 0), (0, 0), (1, 1)))
    return jnp.concatenate(
        [widened[..., shift_y : shift_y + y_count] for shift_y in range(3)], axis=2
    )


def conv_apply(columns, matrix):
    x_count = columns.shape[0] - 2
    z_count = columns.shape[1] - 2
    summed = None
    for shift_x in range(3):
        for shift_z in range(3):
            partial_sum = jnp.einsum(
                "ok,xzky->xzoy",
                matrix[shift_x, shift_z],
                columns[shift_x : shift_x + x_count, shift_z : shift_z + z_count],
                preferred_element_type=jnp.float32,
            )
            summed = partial_sum if summed is None else summed + partial_sum
    return summed


def weight_grad(out_grad, columns):
    x_count = out_grad.shape[0]
    z_count = out_grad.shape[1]
    outer_list = []
    for shift_x in range(3):
        inner_list = []
        for shift_z in range(3):
            inner_list.append(
                jnp.einsum(
                    "xzoy,xzky->ok",
                    out_grad,
                    columns[shift_x : shift_x + x_count, shift_z : shift_z + z_count],
                    preferred_element_type=jnp.float32,
                )
            )
        outer_list.append(jnp.stack(inner_list, axis=0))
    return jnp.stack(outer_list, axis=0)


def as_matrix(weight):
    return weight.reshape(3, 3, weight.shape[2], 3 * weight.shape[4])


def flipped(weight):
    turned = jnp.transpose(jnp.flip(weight, (0, 1, 3)), (0, 1, 4, 3, 2))
    return turned.reshape(3, 3, weight.shape[4], 3 * weight.shape[2])


def silu_grad(values):
    sigma = jax.nn.sigmoid(values)
    return sigma * (1.0 + values * (1.0 - sigma))


def shards_small_chunks(
    kspace,
    measured,
    cotangent,
    coil_maps,
    sample_mask,
    step_size,
    weight_first,
    weight_middle,
    weight_last,
):
    half_len = kspace.shape[3] // 2
    inverse_y = plane_table(half_len, 1.0)
    k_moved, g_moved = (
        lax.all_to_all(kspace, "slab", split_axis=1, concat_axis=2, tiled=True),
        lax.all_to_all(cotangent, "slab", split_axis=1, concat_axis=2, tiled=True),
    )
    k_lines = along_y(k_moved.astype(jnp.float32), inverse_y)
    g_lines = along_y(g_moved.astype(jnp.float32), inverse_y)
    image_full = coil_adjoint(along_z(k_lines, 1.0), coil_maps)
    adjoint_full = coil_adjoint(along_z(g_lines, 1.0), coil_maps)
    summed_image, summed_adjoint = lax.psum((image_full, adjoint_full), ("coil", "half"))
    z_count = summed_image.shape[1] // lax.axis_size(("coil", "half"))
    start = lax.axis_index(("coil", "half")) * z_count
    image = lax.dynamic_slice_in_dim(summed_image, start, z_count, 1)
    adjoint = lax.dynamic_slice_in_dim(summed_adjoint, start, z_count, 1)
    layer_zero = image.astype(jnp.bfloat16)
    cols_zero = columns_of(with_rims(layer_zero))
    pre_first = conv_apply(cols_zero, as_matrix(weight_first))
    act_first = jax.nn.silu(pre_first).astype(jnp.bfloat16)
    cols_first = columns_of(with_rims(act_first))
    pre_middle = conv_apply(cols_first, as_matrix(weight_middle))
    act_middle = jax.nn.silu(pre_middle).astype(jnp.bfloat16)
    cols_middle = columns_of(with_rims(act_middle))
    refined = conv_apply(cols_middle, as_matrix(weight_last)).astype(jnp.bfloat16)
    refined_all = lax.all_gather(refined, ("coil", "half"), axis=1, tiled=True)
    spectra_lines = along_z(coil_expand(refined_all, coil_maps), -1.0)
    spectra_slab = lax.all_to_all(
        spectra_lines.astype(jnp.bfloat16), "slab", split_axis=2, concat_axis=1, tiled=True
    ).astype(spectra_lines.dtype)
    model_term = along_y(spectra_slab, plane_table(half_len, -1.0))
    sampled = sample_mask.astype(jnp.float32)
    sampled = jnp.concatenate([sampled, sampled], axis=1)
    current = kspace.astype(jnp.float32)
    updated = (
        current - step_size[0] * sampled * (current - measured.astype(jnp.float32)) - model_term
    ).astype(jnp.bfloat16)
    grad_out = (-adjoint).astype(jnp.bfloat16)
    grad_last = weight_grad(grad_out, cols_middle)
    back_middle = conv_apply(columns_of(with_rims(grad_out)), flipped(weight_last))
    grad_pre_middle = (back_middle * silu_grad(pre_middle)).astype(jnp.bfloat16)
    grad_middle = weight_grad(grad_pre_middle, cols_first)
    back_first = conv_apply(columns_of(with_rims(grad_pre_middle)), flipped(weight_middle))
    grad_pre_first = (back_first * silu_grad(pre_first)).astype(jnp.bfloat16)
    grad_first = weight_grad(grad_pre_first, cols_zero)
    grad_first, grad_middle, grad_last = lax.psum(
        (grad_first, grad_middle, grad_last), ("slab", "coil", "half")
    )
    return (
        updated,
        grad_first.reshape(weight_first.shape),
        grad_middle.reshape(weight_middle.shape),
        grad_last.reshape(weight_last.shape),
    )


GROUP = ("coil", "half", "slab")


def group_sizes():
    return lax.axis_size("slab"), lax.axis_size("half"), lax.axis_size(GROUP)


def my_position():
    slab_count, half_count, _ = group_sizes()
    coil_half = lax.axis_index("coil") * half_count + lax.axis_index("half")
    return coil_half * slab_count + lax.axis_index("slab")


def device_at(position):
    slab_count, half_count, _ = group_sizes()
    coil_half = lax.div(position, slab_count)
    return {
        "slab": lax.rem(position, slab_count),
        "coil": lax.div(coil_half, half_count),
        "half": lax.rem(coil_half, half_count),
    }


def greet(count, me):
    barrier = pltpu.get_barrier_semaphore()
    for step in range(1, count):
        peer = lax.rem(me + step, count)
        pl.semaphore_signal(
            barrier, inc=1, device_id=device_at(peer), device_id_type=pl.DeviceIdType.MESH
        )
    pl.semaphore_wait(barrier, count - 1)


def send_to(src, dst, send_sem, recv_sem, peer):
    return pltpu.make_async_remote_copy(
        src_ref=src,
        dst_ref=dst,
        send_sem=send_sem,
        recv_sem=recv_sem,
        device_id=device_at(peer),
        device_id_type=pl.DeviceIdType.MESH,
    )


def scatter_slots(count, me, pick, src_ref, dst_ref, send_sem, recv_sem):
    copies = []
    for step in range(1, count):
        peer = lax.rem(me + step, count)
        copy = send_to(
            src_ref.at[pick(peer)], dst_ref.at[me], send_sem.at[step], recv_sem.at[step], peer
        )
        copy.start()
        copies.append(copy)
    dst_ref[me] = src_ref[pick(me)]
    for step in range(1, count):
        source = lax.rem(me + count - step, count)
        send_to(
            src_ref.at[pick(source)],
            dst_ref.at[source],
            send_sem.at[step],
            recv_sem.at[step],
            source,
        ).wait_recv()
    for copy in copies:
        copy.wait_send()


def total_of(values, collective_id):
    _, _, count = group_sizes()

    def kernel(src_ref, dst_ref, parts, own, send_sem, recv_sem, send_two, recv_two):
        me = my_position()
        greet(count, me)
        scatter_slots(count, me, lambda peer: peer, src_ref, parts, send_sem, recv_sem)
        own[0] = jnp.sum(parts[...].astype(jnp.float32), axis=0).astype(own.dtype)
        scatter_slots(count, me, lambda peer: 0, own, dst_ref, send_two, recv_two)

    semaphores = pltpu.SemaphoreType.DMA((count,))
    return pl.pallas_call(
        kernel,
        out_shape=jax.ShapeDtypeStruct(values.shape, values.dtype),
        in_specs=[pl.BlockSpec(memory_space=pltpu.VMEM)],
        out_specs=pl.BlockSpec(memory_space=pltpu.VMEM),
        scratch_shapes=[
            pltpu.VMEM(values.shape, values.dtype),
            pltpu.VMEM((1,) + values.shape[1:], values.dtype),
            semaphores,
            semaphores,
            semaphores,
            semaphores,
        ],
        compiler_params=pltpu.CompilerParams(collective_id=collective_id, has_side_effects=True),
    )(values)


def dft_constants(length):
    position = np.arange(length)
    angles = (position[:, None] * position[None, :] % length) * (2.0 * math.pi / length)
    factor = 1.0 / math.sqrt(length)
    return np.cos(angles) * factor, np.sin(angles) * factor


def plane_constant(length, orient):
    cos_part, sin_part = dft_constants(length)
    return jnp.asarray(
        np.block([[cos_part, orient * sin_part], [-orient * sin_part, cos_part]]), jnp.bfloat16
    )


def lines_y(values, orient):
    return jnp.einsum(
        "cxzk,kw->cxzw",
        values,
        plane_constant(values.shape[3] // 2, orient),
        preferred_element_type=jnp.float32,
    )


def lines_z(values, orient):
    length = values.shape[2]
    half_len = values.shape[3] // 2
    cos_part, sin_part = dft_constants(length)
    mixture = jnp.einsum(
        "wz,cxzk->cxwk",
        jnp.asarray(np.concatenate([cos_part, sin_part], axis=0), jnp.bfloat16),
        values,
        preferred_element_type=jnp.float32,
    )
    direct = mixture[:, :, :length]
    crossed = mixture[:, :, length:]
    turned = jnp.concatenate(
        [-orient * crossed[..., half_len:], orient * crossed[..., :half_len]], axis=-1
    )
    return direct + turned


def band_of(x_count):
    shift = np.arange(3)[:, None, None]
    source = np.arange(x_count)[None, :, None]
    target = np.arange(x_count)[None, None, :]
    return (source == target + shift - 1).astype(np.float32)


def banded(weight, x_count):
    band = jnp.asarray(band_of(x_count), jnp.bfloat16)
    wide = jnp.einsum("dzoyi,dab->zyaibo", weight, band, preferred_element_type=jnp.bfloat16)
    return wide.reshape(3, 3, x_count * weight.shape[4], x_count * weight.shape[2])


def halves_padded(values, wide):
    half_len = values.shape[-1] // 2
    edge = [(0, 0)] * (values.ndim - 1) + [(0, wide - half_len)]
    return jnp.concatenate(
        [jnp.pad(values[..., :half_len], edge), jnp.pad(values[..., half_len:], edge)], axis=-1
    )


def two_parts(table):
    high = table.astype(ml_dtypes.bfloat16)
    low = (table - high.astype(np.float64)).astype(ml_dtypes.bfloat16)
    return jnp.asarray(high), jnp.asarray(low)


def rounded_parts(values):
    high = values.astype(jnp.bfloat16)
    return high, (values - high.astype(jnp.float32)).astype(jnp.bfloat16)


def dot(left, right):
    return jnp.dot(left, right, preferred_element_type=jnp.float32)


def images(kspace, cotangent, coil_maps, weights, rim, collective_id):
    slab_count, _, count = group_sizes()
    coil_count, x_count, slab_rows, width = kspace.shape
    length = slab_count * slab_rows
    half_len = width // 2
    wide = -(-half_len // 128) * 128
    z_count = length // count
    window = z_count + 2 * rim
    tall = length + 2 * rim

    cos_y, sin_y = dft_constants(half_len)
    table_y = np.zeros((width, 2 * wide))
    table_y[:half_len, :half_len] = cos_y
    table_y[:half_len, wide : wide + half_len] = sin_y
    table_y[half_len:, :half_len] = -sin_y
    table_y[half_len:, wide : wide + half_len] = cos_y
    cos_z, sin_z = dft_constants(length)
    table_z = np.zeros((2 * tall, length))
    table_z[rim : rim + length] = cos_z
    table_z[tall + rim : tall + rim + length] = sin_z
    maps = halves_padded(coil_maps[:, 0], wide)
    maps = jnp.pad(maps, ((0, 0), (rim, rim), (0, 0)))

    def kernel(
        k_ref, g_ref, maps_ref, yh_ref, yl_ref, zh_ref, zl_ref, first_ref, middle_ref, last_ref,
        adjoint_ref, refined_ref, taps_zero, taps_first, taps_middle, pre_first, pre_middle,
        image_ref, moved, lines, total, slots, parts, planes, stacked, refined_slots,
        send_one, recv_one, send_two, recv_two, send_three, recv_three,
    ):
        me = my_position()
        slab = lax.axis_index("slab")
        greet(count, me)

        def moving(which, step, source_ref, sending):
            offset = step if sending else slab_count - step
            peer = lax.rem(slab + offset, slab_count)
            return pltpu.make_async_remote_copy(
                src_ref=source_ref.at[:, peer],
                dst_ref=moved.at[which, slab if sending else peer],
                send_sem=send_one.at[which, step],
                recv_sem=recv_one.at[which, step],
                device_id={"slab": peer},
                device_id_type=pl.DeviceIdType.MESH,
            )

        def spreading(which, step, sending):
            peer = lax.rem(me + (step if sending else count - step), count)
            return send_to(
                slots.at[which, peer],
                parts.at[which, me if sending else peer],
                send_two.at[which, step],
                recv_two.at[which, step],
                peer,
            )

        sources = (k_ref, g_ref)
        outs = (image_ref, adjoint_ref)

        def refining(step, sending):
            peer = lax.rem(me + (step if sending else count - step), count)
            return send_to(
                refined_slots.at[lax.rem(peer, slab_count)],
                refined_ref.at[me if sending else peer],
                send_three.at[step],
                recv_three.at[step],
                peer,
            )

        def start_moving(which):
            for step in range(1, slab_count):
                moving(which, step, sources[which], True).start()
            moved[which, slab] = sources[which][:, slab]

        def start_spreading(which):
            for step in range(1, slab_count):
                moving(which, step, sources[which], False).wait_recv()
            for block in range(slab_count):
                rows = moved[which, block].reshape(coil_count * slab_rows, width)
                product = dot(rows, yh_ref[...]) + dot(rows, yl_ref[...])
                lines[:, block * slab_rows : (block + 1) * slab_rows] = product.reshape(
                    coil_count, slab_rows, 2 * wide
                )

            @pl.loop(0, coil_count)
            def _(coil):
                high, low = rounded_parts(lines[coil])
                mixture = dot(zh_ref[...], high) + dot(zh_ref[...], low) + dot(zl_ref[...], high)
                line_real = mixture[:tall, :wide] - mixture[tall:, wide:]
                line_imag = mixture[:tall, wide:] + mixture[tall:, :wide]
                coil_map = maps_ref[coil].astype(jnp.float32)
                map_real, map_imag = coil_map[:, :wide], coil_map[:, wide:]
                real_part = map_real * line_real + map_imag * line_imag
                imag_part = map_real * line_imag - map_imag * line_real
                fresh = jnp.concatenate([real_part, imag_part], axis=1)
                total[...] = jnp.where(coil == 0, fresh, total[...] + fresh)

            for spot in range(count):
                slots[which, spot] = total[spot * z_count : spot * z_count + window].astype(
                    jnp.bfloat16
                )
            for step in range(1, count):
                spreading(which, step, True).start()
            parts[which, me] = slots[which, me]

        def finish_spreading(which):
            for step in range(1, count):
                spreading(which, step, False).wait_recv()
            for spot in range(slab_count):
                summed = parts[which, spot].astype(jnp.float32)
                for other in range(spot + slab_count, count, slab_count):
                    summed = summed + parts[which, other].astype(jnp.float32)
                summed = summed.astype(jnp.bfloat16).astype(jnp.float32)
                outs[which][:, 2 * spot, :] = summed[:, :wide]
                outs[which][:, 2 * spot + 1, :] = summed[:, wide:]

        start_moving(0)
        start_spreading(0)
        start_moving(1)
        finish_spreading(0)

        @pl.loop(0, z_count + 6)
        def _(row):
            fill_taps(taps_zero, row, pixels_of(image_ref[row + 1], half_len))

        @pl.loop(0, z_count + 4)
        def _(row):
            pre = conv_row(taps_zero, first_ref, row)
            pre_first[row] = pre
            act = pre / (1.0 + jnp.exp(-pre))
            fill_taps(
                taps_first, row, jnp.where(row_inside(row - 2, me, z_count, length), act, 0.0)
            )

        @pl.loop(0, z_count + 2)
        def _(row):
            pre = conv_row(taps_first, middle_ref, row)
            pre_middle[row] = pre
            act = pre / (1.0 + jnp.exp(-pre))
            fill_taps(
                taps_middle, row, jnp.where(row_inside(row - 1, me, z_count, length), act, 0.0)
            )

        @pl.loop(0, z_count)
        def _(row):
            planes[row] = conv_row(taps_middle, last_ref, row).T[: 2 * slab_count]

        for spot in range(slab_count):
            for row in range(z_count):
                stacked[spot, 2 * row : 2 * row + 2] = planes[row, 2 * spot : 2 * spot + 2]
            refined_slots[spot] = stacked[spot].astype(jnp.bfloat16)
        for step in range(1, count):
            refining(step, True).start()
        refined_ref[me] = refined_slots[slab]
        start_spreading(1)
        for step in range(1, count):
            refining(step, False).wait_recv()
        finish_spreading(1)
        for which in range(2):
            for step in range(1, slab_count):
                moving(which, step, sources[which], True).wait_send()
            for step in range(1, count):
                spreading(which, step, True).wait_send()
        for step in range(1, count):
            refining(step, True).wait_send()

    def taps(extra):
        return jax.ShapeDtypeStruct((z_count + extra, half_len, 3 * LANES), jnp.bfloat16)

    def full(extra):
        return jax.ShapeDtypeStruct((z_count + extra, half_len, LANES), jnp.float32)

    shape = jax.ShapeDtypeStruct((window, 2 * slab_count, wide), jnp.float32)
    whole = pl.BlockSpec(memory_space=pltpu.VMEM)
    return pl.pallas_call(
        kernel,
        out_shape=(
            shape,
            jax.ShapeDtypeStruct((count, 2 * z_count, half_len), jnp.bfloat16),
            taps(6), taps(4), taps(2), full(4), full(2),
        ),
        in_specs=[whole] * 10,
        out_specs=(whole,) * 7,
        scratch_shapes=[
            pltpu.VMEM((window, 2 * slab_count, wide), jnp.float32),
            pltpu.VMEM((2, slab_count, coil_count, slab_rows, width), jnp.bfloat16),
            pltpu.VMEM((coil_count, length, 2 * wide), jnp.float32),
            pltpu.VMEM((tall, 2 * wide), jnp.float32),
            pltpu.VMEM((2, count, window, 2 * wide), jnp.bfloat16),
            pltpu.VMEM((2, count, window, 2 * wide), jnp.bfloat16),
            pltpu.VMEM((z_count, 2 * slab_count, half_len), jnp.float32),
            pltpu.VMEM((slab_count, 2 * z_count, half_len), jnp.float32),
            pltpu.VMEM((slab_count, 2 * z_count, half_len), jnp.bfloat16),
            pltpu.SemaphoreType.DMA((2, slab_count)),
            pltpu.SemaphoreType.DMA((2, slab_count)),
            pltpu.SemaphoreType.DMA((2, count)),
            pltpu.SemaphoreType.DMA((2, count)),
            pltpu.SemaphoreType.DMA((count,)),
            pltpu.SemaphoreType.DMA((count,)),
        ],
        compiler_params=pltpu.CompilerParams(
            collective_id=collective_id, has_side_effects=True, vmem_limit_bytes=56 * 2**20
        ),
    )(kspace, cotangent, maps, *two_parts(table_y), *two_parts(table_z), *weights)


LANES = 128


def tap_rows(kernel):
    edge = [(0, 0), (0, 0), (0, LANES - kernel.shape[2]), (0, LANES - kernel.shape[3])]
    return jnp.pad(kernel, edge).reshape(3, 3 * LANES, LANES)


def back_taps(kernel):
    return jnp.transpose(jnp.flip(kernel, (0, 1)), (0, 1, 3, 2))


def pixels_of(plane, y_count):
    filler = jnp.zeros((LANES - plane.shape[0], plane.shape[1]), plane.dtype)
    return jnp.concatenate([plane, filler], axis=0).T[:y_count]


def fill_taps(taps_ref, row, values):
    y_count = values.shape[0]
    position = lax.broadcasted_iota(jnp.int32, values.shape, 0)
    before = jnp.where(position == 0, 0.0, pltpu.roll(values, 1, 0))
    after = jnp.where(position == y_count - 1, 0.0, pltpu.roll(values, y_count - 1, 0))
    taps_ref[row, :, :LANES] = before.astype(jnp.bfloat16)
    taps_ref[row, :, LANES : 2 * LANES] = values.astype(jnp.bfloat16)
    taps_ref[row, :, 2 * LANES :] = after.astype(jnp.bfloat16)


def conv_row(taps_ref, weight_ref, row):
    summed = dot(taps_ref[row], weight_ref[0])
    for shift_z in range(1, 3):
        summed = summed + dot(taps_ref[row + shift_z], weight_ref[shift_z])
    return summed


def row_inside(row, me, z_count, length):
    place = me * z_count + row
    return jnp.logical_and(place >= 0, place < length)


def backward_layers(
    adjoint, taps_zero, taps_first, taps_middle, pre_first, pre_middle, weights,
    z_count, length, y_count, x_count, slot_rows,
):
    channels = LANES // x_count
    few = adjoint.shape[1]

    def kernel(
        adjoint_ref, zero_ref, first_ref, middle_ref, pre_first_ref, pre_middle_ref,
        back_middle_ref, back_last_ref, rounded_ref, out_taps, grad_taps, sums, out_ref,
    ):
        me = my_position()

        @pl.loop(0, z_count + 4)
        def _(row):
            fill_taps(out_taps, row, -pixels_of(adjoint_ref[row + 2], y_count))

        @pl.loop(0, z_count + 2)
        def _(row):
            grad = conv_row(out_taps, back_last_ref, row) * silu_grad(pre_middle_ref[row])
            fill_taps(
                grad_taps, row, jnp.where(row_inside(row - 1, me, z_count, length), grad, 0.0)
            )

        sums[...] = jnp.zeros_like(sums)

        def gather(which, grad, taps_ref, row):
            for shift_z in range(3):
                sums[which, shift_z] += lax.dot_general(
                    grad,
                    taps_ref[row + shift_z],
                    (((0,), (0,)), ((), ())),
                    preferred_element_type=jnp.float32,
                )

        @pl.loop(0, z_count)
        def _(row):
            grad = conv_row(grad_taps, back_middle_ref, row) * silu_grad(pre_first_ref[row + 2])
            gather(0, grad.astype(jnp.bfloat16), zero_ref, row + 2)
            gather(1, grad_taps[row + 1, :, LANES : 2 * LANES], first_ref, row + 1)
            gather(2, out_taps[row + 2, :, LANES : 2 * LANES], middle_ref, row)

        out_ref[...] = jnp.zeros_like(out_ref)
        group = lax.broadcasted_iota(jnp.int32, (channels, LANES), 1) // channels
        for shift_z in range(3):
            for shift_y in range(3):
                tap = shift_z * 3 + shift_y
                lanes = slice(shift_y * LANES, (shift_y + 1) * LANES)
                square = sums[1, shift_z, :, lanes]
                folded = jnp.zeros((channels, LANES), jnp.float32)
                for shift_x in range(3):
                    picked = jnp.zeros((channels, LANES), jnp.float32)
                    for spot in range(x_count):
                        picked = picked + jnp.where(
                            group == spot + shift_x - 1,
                            square[spot * channels : (spot + 1) * channels],
                            0.0,
                        )
                    turn = LANES // 2
                    while turn >= channels:
                        picked = picked + pltpu.roll(picked, turn, 1)
                        turn //= 2
                    folded = jnp.where(group == shift_x, picked, folded)
                out_ref[tap * channels : (tap + 1) * channels] = folded
                base = 9 * channels + tap * few
                out_ref[base : base + few] = sums[0, shift_z, :, lanes].T[:few]
                base = base + 9 * few
                out_ref[base : base + few] = sums[2, shift_z, :few, lanes]
        rounded_ref[...] = out_ref[...].astype(jnp.bfloat16)

    whole = pl.BlockSpec(memory_space=pltpu.VMEM)
    return pl.pallas_call(
        kernel,
        out_shape=jax.ShapeDtypeStruct((slot_rows, LANES), jnp.bfloat16),
        in_specs=[whole] * 8,
        out_specs=whole,
        scratch_shapes=[
            pltpu.VMEM((z_count + 4, y_count, 3 * LANES), jnp.bfloat16),
            pltpu.VMEM((z_count + 2, y_count, 3 * LANES), jnp.bfloat16),
            pltpu.VMEM((3, 3, LANES, 3 * LANES), jnp.float32),
            pltpu.VMEM((slot_rows, LANES), jnp.float32),
        ],
        compiler_params=pltpu.CompilerParams(vmem_limit_bytes=56 * 2**20),
    )(adjoint, taps_zero, taps_first, taps_middle, pre_first, pre_middle, *weights)


def band_sums(pairs, x_count):
    pieces = []
    for shift_x in range(3):
        picked = [
            pairs(target + shift_x - 1, target)
            for target in range(x_count)
            if 0 <= target + shift_x - 1 < x_count
        ]
        pieces.append(functools.reduce(jnp.add, picked))
    return jnp.stack(pieces)


def shards(
    kspace,
    measured,
    cotangent,
    coil_maps,
    sample_mask,
    step_size,
    weight_first,
    weight_middle,
    weight_last,
):
    slab_count, _, count = group_sizes()
    length = coil_maps.shape[2]
    half_len = kspace.shape[3] // 2
    z_count = length // count
    rim = 4
    lanes = slab_count * weight_middle.shape[2]
    if coil_maps.shape[1] != 1 or length % count or z_count % 8 or lanes != LANES or half_len % 16:
        return shards_small_chunks(
            kspace,
            measured,
            cotangent,
            coil_maps,
            sample_mask,
            step_size,
            weight_first,
            weight_middle,
            weight_last,
        )
    x_count = slab_count

    kernel_middle = banded(weight_middle, x_count)
    kernel_last = banded(weight_last, x_count)
    adjoint, refined_all, *kept = images(
        kspace,
        cotangent,
        coil_maps,
        (
            tap_rows(banded(weight_first, x_count)),
            tap_rows(kernel_middle),
            tap_rows(kernel_last),
        ),
        rim,
        0,
    )
    refined_all = refined_all.reshape(1, length, 2, half_len)

    spectra = lines_z(coil_expand(refined_all, coil_maps).astype(jnp.bfloat16), -1.0)
    spectra_slab = lax.all_to_all(
        spectra.astype(jnp.bfloat16), "slab", split_axis=2, concat_axis=1, tiled=True
    )
    model_term = lines_y(spectra_slab, -1.0)
    sampled = sample_mask.astype(jnp.float32)
    sampled = jnp.concatenate([sampled, sampled], axis=1)
    current = kspace.astype(jnp.float32)
    updated = (
        current - step_size[0] * sampled * (current - measured.astype(jnp.float32)) - model_term
    ).astype(jnp.bfloat16)

    channels = LANES // x_count
    few = 2 * x_count
    used = 9 * (channels + 2 * few)
    slot_rows = -(-used // (16 * count)) * 16 * count
    local = backward_layers(
        adjoint,
        *kept,
        (tap_rows(back_taps(kernel_middle)), tap_rows(back_taps(kernel_last))),
        z_count,
        length,
        half_len,
        x_count,
        slot_rows,
    )
    total = total_of(local.reshape(count, -1, LANES), 3)
    total = total.reshape(slot_rows, LANES).astype(jnp.float32)
    wide_rows = 9 * channels
    middle = total[:wide_rows].reshape(3, 3, channels, x_count, channels)[:, :, :, :3]
    first = total[wide_rows : wide_rows + 9 * few].reshape(3, 3, x_count, 2, x_count, channels)
    last = total[wide_rows + 9 * few : used].reshape(3, 3, x_count, 2, x_count, channels)
    grad_middle = jnp.transpose(middle, (3, 0, 2, 1, 4))
    grad_first = band_sums(lambda source, target: first[:, :, source, :, target], x_count)
    grad_last = band_sums(lambda source, target: last[:, :, target, :, source], x_count)
    return (
        updated,
        jnp.transpose(grad_first, (0, 1, 4, 2, 3)),
        grad_middle,
        jnp.transpose(grad_last, (0, 1, 3, 2, 4)),
    )


def solution(mesh):
    return jax.shard_map(
        shards,
        mesh=mesh,
        in_specs=(
            P(("grp", "coil", "half"), None, "slab", None),
            P(("grp", "coil", "half"), None, "slab", None),
            P(("grp", "coil", "half"), None, "slab", None),
            P(("grp", "coil", "half"), "slab", None, None),
            P(("grp", "slab"), None),
            P(),
            P(),
            P(),
            P(),
        ),
        out_specs=(
            P(("grp", "coil", "half"), None, "slab", None),
            P("grp", None, None, None, None),
            P("grp", None, None, None, None),
            P("grp", None, None, None, None),
        ),
        check_vma=False,
    )
```

```python
import functools
import math

import jax
import jax.numpy as jnp
import ml_dtypes
import numpy as np
from jax import lax
from jax.experimental import pallas as pl
from jax.experimental.pallas import tpu as pltpu
from jax.sharding import PartitionSpec as P


def with_halo(block, sides, width):
    for axis, dim in sides:
        count = lax.axis_size(axis)
        forward = [(i, i + 1) for i in range(count - 1)]
        backward = [(target, source) for source, target in forward]
        low = lax.ppermute(
            lax.slice_in_dim(block, block.shape[dim] - width, None, axis=dim), axis, forward
        )
        high = lax.ppermute(lax.slice_in_dim(block, 0, width, axis=dim), axis, backward)
        block = jnp.concatenate([low, block, high], axis=dim)
    return block


def dft_parts(length):
    position = lax.iota(jnp.int32, length)
    product = position[:, None] * position[None, :] % length
    angles = product.astype(jnp.float32) * (2.0 * math.pi / length)
    factor = 1.0 / math.sqrt(length)
    return (jnp.cos(angles) * factor, jnp.sin(angles) * factor)


def plane_table(length, orient):
    cos_part, sin_part = dft_parts(length)
    upper_rows = jnp.concatenate([cos_part, orient * sin_part], axis=1)
    lower_rows = jnp.concatenate([-orient * sin_part, cos_part], axis=1)
    return jnp.concatenate([upper_rows, lower_rows], axis=0)


def along_y(values, table):
    return jnp.einsum(
        "cxzk,kw->cxzw",
        values,
        table,
        precision=lax.Precision.HIGH,
        preferred_element_type=jnp.float32,
    )


def along_z(values, orient):
    length = values.shape[2]
    half_len = values.shape[3] // 2
    cos_part, sin_part = dft_parts(length)
    stacked = jnp.concatenate([cos_part, sin_part], axis=0)
    mixture = jnp.einsum(
        "wz,cxzk->cxwk",
        stacked,
        values,
        precision=lax.Precision.HIGH,
        preferred_element_type=jnp.float32,
    )
    direct = mixture[:, :, :length]
    crossed = mixture[:, :, length:]
    turned = jnp.concatenate(
        [-orient * crossed[..., half_len:], orient * crossed[..., :half_len]], axis=-1
    )
    return direct + turned


def coil_adjoint(lines, coil_maps):
    half_len = lines.shape[3] // 2
    map_values = coil_maps.astype(jnp.float32)
    map_real = map_values[..., :half_len]
    map_imag = map_values[..., half_len:]
    line_real = lines[..., :half_len]
    line_imag = lines[..., half_len:]
    real_sum = jnp.sum(map_real * line_real + map_imag * line_imag, axis=0)
    imag_sum = jnp.sum(map_real * line_imag - map_imag * line_real, axis=0)
    return jnp.stack([real_sum, imag_sum], axis=2)


def coil_expand(image, coil_maps):
    half_len = coil_maps.shape[3] // 2
    map_values = coil_maps.astype(jnp.float32)
    map_real = map_values[..., :half_len]
    map_imag = map_values[..., half_len:]
    image_real = image[:, :, 0].astype(jnp.float32)
    image_imag = image[:, :, 1].astype(jnp.float32)
    out_real = map_real * image_real - map_imag * image_imag
    out_imag = map_real * image_imag + map_imag * image_real
    return jnp.concatenate([out_real, out_imag], axis=-1)


def with_rims(values):
    return with_halo(values, (("slab", 0), (("coil", "half"), 1)), 1)


def columns_of(padded):
    y_count = padded.shape[3]
    widened = jnp.pad(padded, ((0, 0), (0, 0), (0, 0), (1, 1)))
    return jnp.concatenate(
        [widened[..., shift_y : shift_y + y_count] for shift_y in range(3)], axis=2
    )


def conv_apply(columns, matrix):
    x_count = columns.shape[0] - 2
    z_count = columns.shape[1] - 2
    summed = None
    for shift_x in range(3):
        for shift_z in range(3):
            partial_sum = jnp.einsum(
                "ok,xzky->xzoy",
                matrix[shift_x, shift_z],
                columns[shift_x : shift_x + x_count, shift_z : shift_z + z_count],
                preferred_element_type=jnp.float32,
            )
            summed = partial_sum if summed is None else summed + partial_sum
    return summed


def weight_grad(out_grad, columns):
    x_count = out_grad.shape[0]
    z_count = out_grad.shape[1]
    outer_list = []
    for shift_x in range(3):
        inner_list = []
        for shift_z in range(3):
            inner_list.append(
                jnp.einsum(
                    "xzoy,xzky->ok",
                    out_grad,
                    columns[shift_x : shift_x + x_count, shift_z : shift_z + z_count],
                    preferred_element_type=jnp.float32,
                )
            )
        outer_list.append(jnp.stack(inner_list, axis=0))
    return jnp.stack(outer_list, axis=0)


def as_matrix(weight):
    return weight.reshape(3, 3, weight.shape[2], 3 * weight.shape[4])


def flipped(weight):
    turned = jnp.transpose(jnp.flip(weight, (0, 1, 3)), (0, 1, 4, 3, 2))
    return turned.reshape(3, 3, weight.shape[4], 3 * weight.shape[2])


def silu_grad(values):
    sigma = jax.nn.sigmoid(values)
    return sigma * (1.0 + values * (1.0 - sigma))


def shards_small_chunks(
    kspace,
    measured,
    cotangent,
    coil_maps,
    sample_mask,
    step_size,
    weight_first,
    weight_middle,
    weight_last,
):
    half_len = kspace.shape[3] // 2
    inverse_y = plane_table(half_len, 1.0)
    k_moved, g_moved = (
        lax.all_to_all(kspace, "slab", split_axis=1, concat_axis=2, tiled=True),
        lax.all_to_all(cotangent, "slab", split_axis=1, concat_axis=2, tiled=True),
    )
    k_lines = along_y(k_moved.astype(jnp.float32), inverse_y)
    g_lines = along_y(g_moved.astype(jnp.float32), inverse_y)
    image_full = coil_adjoint(along_z(k_lines, 1.0), coil_maps)
    adjoint_full = coil_adjoint(along_z(g_lines, 1.0), coil_maps)
    summed_image, summed_adjoint = lax.psum((image_full, adjoint_full), ("coil", "half"))
    z_count = summed_image.shape[1] // lax.axis_size(("coil", "half"))
    start = lax.axis_index(("coil", "half")) * z_count
    image = lax.dynamic_slice_in_dim(summed_image, start, z_count, 1)
    adjoint = lax.dynamic_slice_in_dim(summed_adjoint, start, z_count, 1)
    layer_zero = image.astype(jnp.bfloat16)
    cols_zero = columns_of(with_rims(layer_zero))
    pre_first = conv_apply(cols_zero, as_matrix(weight_first))
    act_first = jax.nn.silu(pre_first).astype(jnp.bfloat16)
    cols_first = columns_of(with_rims(act_first))
    pre_middle = conv_apply(cols_first, as_matrix(weight_middle))
    act_middle = jax.nn.silu(pre_middle).astype(jnp.bfloat16)
    cols_middle = columns_of(with_rims(act_middle))
    refined = conv_apply(cols_middle, as_matrix(weight_last)).astype(jnp.bfloat16)
    refined_all = lax.all_gather(refined, ("coil", "half"), axis=1, tiled=True)
    spectra_lines = along_z(coil_expand(refined_all, coil_maps), -1.0)
    spectra_slab = lax.all_to_all(
        spectra_lines.astype(jnp.bfloat16), "slab", split_axis=2, concat_axis=1, tiled=True
    ).astype(spectra_lines.dtype)
    model_term = along_y(spectra_slab, plane_table(half_len, -1.0))
    sampled = sample_mask.astype(jnp.float32)
    sampled = jnp.concatenate([sampled, sampled], axis=1)
    current = kspace.astype(jnp.float32)
    updated = (
        current - step_size[0] * sampled * (current - measured.astype(jnp.float32)) - model_term
    ).astype(jnp.bfloat16)
    grad_out = (-adjoint).astype(jnp.bfloat16)
    grad_last = weight_grad(grad_out, cols_middle)
    back_middle = conv_apply(columns_of(with_rims(grad_out)), flipped(weight_last))
    grad_pre_middle = (back_middle * silu_grad(pre_middle)).astype(jnp.bfloat16)
    grad_middle = weight_grad(grad_pre_middle, cols_first)
    back_first = conv_apply(columns_of(with_rims(grad_pre_middle)), flipped(weight_middle))
    grad_pre_first = (back_first * silu_grad(pre_first)).astype(jnp.bfloat16)
    grad_first = weight_grad(grad_pre_first, cols_zero)
    grad_first, grad_middle, grad_last = lax.psum(
        (grad_first, grad_middle, grad_last), ("slab", "coil", "half")
    )
    return (
        updated,
        grad_first.reshape(weight_first.shape),
        grad_middle.reshape(weight_middle.shape),
        grad_last.reshape(weight_last.shape),
    )


GROUP = ("coil", "half", "slab")


def group_sizes():
    return lax.axis_size("slab"), lax.axis_size("half"), lax.axis_size(GROUP)


def my_position():
    slab_count, half_count, _ = group_sizes()
    coil_half = lax.axis_index("coil") * half_count + lax.axis_index("half")
    return coil_half * slab_count + lax.axis_index("slab")


def device_at(position):
    slab_count, half_count, _ = group_sizes()
    coil_half = lax.div(position, slab_count)
    return {
        "slab": lax.rem(position, slab_count),
        "coil": lax.div(coil_half, half_count),
        "half": lax.rem(coil_half, half_count),
    }


def greet(count, me):
    barrier = pltpu.get_barrier_semaphore()
    for step in range(1, count):
        peer = lax.rem(me + step, count)
        pl.semaphore_signal(
            barrier, inc=1, device_id=device_at(peer), device_id_type=pl.DeviceIdType.MESH
        )
    pl.semaphore_wait(barrier, count - 1)


def send_to(src, dst, send_sem, recv_sem, peer):
    return pltpu.make_async_remote_copy(
        src_ref=src,
        dst_ref=dst,
        send_sem=send_sem,
        recv_sem=recv_sem,
        device_id=device_at(peer),
        device_id_type=pl.DeviceIdType.MESH,
    )


def scatter_slots(count, me, pick, src_ref, dst_ref, send_sem, recv_sem):
    copies = []
    for step in range(1, count):
        peer = lax.rem(me + step, count)
        copy = send_to(
            src_ref.at[pick(peer)], dst_ref.at[me], send_sem.at[step], recv_sem.at[step], peer
        )
        copy.start()
        copies.append(copy)
    dst_ref[me] = src_ref[pick(me)]
    for step in range(1, count):
        source = lax.rem(me + count - step, count)
        send_to(
            src_ref.at[pick(source)],
            dst_ref.at[source],
            send_sem.at[step],
            recv_sem.at[step],
            source,
        ).wait_recv()
    for copy in copies:
        copy.wait_send()


def total_of(values, collective_id):
    _, _, count = group_sizes()

    def kernel(src_ref, dst_ref, parts, own, send_sem, recv_sem, send_two, recv_two):
        me = my_position()
        greet(count, me)
        scatter_slots(count, me, lambda peer: peer, src_ref, parts, send_sem, recv_sem)
        own[0] = jnp.sum(parts[...].astype(jnp.float32), axis=0).astype(own.dtype)
        scatter_slots(count, me, lambda peer: 0, own, dst_ref, send_two, recv_two)

    semaphores = pltpu.SemaphoreType.DMA((count,))
    return pl.pallas_call(
        kernel,
        out_shape=jax.ShapeDtypeStruct(values.shape, values.dtype),
        in_specs=[pl.BlockSpec(memory_space=pltpu.VMEM)],
        out_specs=pl.BlockSpec(memory_space=pltpu.VMEM),
        scratch_shapes=[
            pltpu.VMEM(values.shape, values.dtype),
            pltpu.VMEM((1,) + values.shape[1:], values.dtype),
            semaphores,
            semaphores,
            semaphores,
            semaphores,
        ],
        compiler_params=pltpu.CompilerParams(collective_id=collective_id, has_side_effects=True),
    )(values)


def dft_constants(length):
    position = np.arange(length)
    angles = (position[:, None] * position[None, :] % length) * (2.0 * math.pi / length)
    factor = 1.0 / math.sqrt(length)
    return np.cos(angles) * factor, np.sin(angles) * factor


def plane_constant(length, orient):
    cos_part, sin_part = dft_constants(length)
    return jnp.asarray(
        np.block([[cos_part, orient * sin_part], [-orient * sin_part, cos_part]]), jnp.bfloat16
    )


def lines_y(values, orient):
    return jnp.einsum(
        "cxzk,kw->cxzw",
        values,
        plane_constant(values.shape[3] // 2, orient),
        preferred_element_type=jnp.float32,
    )


def lines_z(values, orient):
    length = values.shape[2]
    half_len = values.shape[3] // 2
    cos_part, sin_part = dft_constants(length)
    mixture = jnp.einsum(
        "wz,cxzk->cxwk",
        jnp.asarray(np.concatenate([cos_part, sin_part], axis=0), jnp.bfloat16),
        values,
        preferred_element_type=jnp.float32,
    )
    direct = mixture[:, :, :length]
    crossed = mixture[:, :, length:]
    turned = jnp.concatenate(
        [-orient * crossed[..., half_len:], orient * crossed[..., :half_len]], axis=-1
    )
    return direct + turned


def band_of(x_count):
    shift = np.arange(3)[:, None, None]
    source = np.arange(x_count)[None, :, None]
    target = np.arange(x_count)[None, None, :]
    return (source == target + shift - 1).astype(np.float32)


def banded(weight, x_count):
    band = jnp.asarray(band_of(x_count), jnp.bfloat16)
    wide = jnp.einsum("dzoyi,dab->zyaibo", weight, band, preferred_element_type=jnp.bfloat16)
    return wide.reshape(3, 3, x_count * weight.shape[4], x_count * weight.shape[2])


def halves_padded(values, wide):
    half_len = values.shape[-1] // 2
    edge = [(0, 0)] * (values.ndim - 1) + [(0, wide - half_len)]
    return jnp.concatenate(
        [jnp.pad(values[..., :half_len], edge), jnp.pad(values[..., half_len:], edge)], axis=-1
    )


def two_parts(table):
    high = table.astype(ml_dtypes.bfloat16)
    low = (table - high.astype(np.float64)).astype(ml_dtypes.bfloat16)
    return jnp.asarray(high), jnp.asarray(low)


def rounded_parts(values):
    high = values.astype(jnp.bfloat16)
    return high, (values - high.astype(jnp.float32)).astype(jnp.bfloat16)


def dot(left, right):
    return jnp.dot(left, right, preferred_element_type=jnp.float32)


def images(kspace, cotangent, coil_maps, weights, rim, collective_id):
    slab_count, _, count = group_sizes()
    coil_count, x_count, slab_rows, width = kspace.shape
    length = slab_count * slab_rows
    half_len = width // 2
    wide = -(-half_len // 128) * 128
    z_count = length // count
    window = z_count + 2 * rim
    tall = length + 2 * rim

    cos_y, sin_y = dft_constants(half_len)
    table_y = np.zeros((width, 2 * wide))
    table_y[:half_len, :half_len] = cos_y
    table_y[:half_len, wide : wide + half_len] = sin_y
    table_y[half_len:, :half_len] = -sin_y
    table_y[half_len:, wide : wide + half_len] = cos_y
    cos_z, sin_z = dft_constants(length)
    table_z = np.zeros((2 * tall, length))
    table_z[rim : rim + length] = cos_z
    table_z[tall + rim : tall + rim + length] = sin_z
    maps = halves_padded(coil_maps[:, 0], wide)
    maps = jnp.pad(maps, ((0, 0), (rim, rim), (0, 0)))

    def kernel(
        k_ref, g_ref, maps_ref, yh_ref, yl_ref, zh_ref, zl_ref, first_ref, middle_ref, last_ref,
        adjoint_ref, refined_ref, taps_zero, taps_first, taps_middle, pre_first, pre_middle,
        image_ref, moved, lines, total, slots, parts, planes, stacked, refined_slots,
        send_one, recv_one, send_two, recv_two, send_three, recv_three,
    ):
        me = my_position()
        slab = lax.axis_index("slab")
        greet(count, me)

        def moving(which, step, source_ref, sending):
            offset = step if sending else slab_count - step
            peer = lax.rem(slab + offset, slab_count)
            return pltpu.make_async_remote_copy(
                src_ref=source_ref.at[:, peer],
                dst_ref=moved.at[which, slab if sending else peer],
                send_sem=send_one.at[which, step],
                recv_sem=recv_one.at[which, step],
                device_id={"slab": peer},
                device_id_type=pl.DeviceIdType.MESH,
            )

        def spreading(which, step, sending):
            peer = lax.rem(me + (step if sending else count - step), count)
            return send_to(
                slots.at[which, peer],
                parts.at[which, me if sending else peer],
                send_two.at[which, step],
                recv_two.at[which, step],
                peer,
            )

        sources = (k_ref, g_ref)
        outs = (image_ref, adjoint_ref)

        def refining(step, sending):
            peer = lax.rem(me + (step if sending else count - step), count)
            return send_to(
                refined_slots.at[lax.rem(peer, slab_count)],
                refined_ref.at[me if sending else peer],
                send_three.at[step],
                recv_three.at[step],
                peer,
            )

        def start_moving(which):
            for step in range(1, slab_count):
                moving(which, step, sources[which], True).start()
            moved[which, slab] = sources[which][:, slab]

        def start_spreading(which):
            for step in range(1, slab_count):
                moving(which, step, sources[which], False).wait_recv()
            for block in range(slab_count):
                rows = moved[which, block].reshape(coil_count * slab_rows, width)
                product = dot(rows, yh_ref[...]) + dot(rows, yl_ref[...])
                lines[:, block * slab_rows : (block + 1) * slab_rows] = product.reshape(
                    coil_count, slab_rows, 2 * wide
                )

            @pl.loop(0, coil_count)
            def _(coil):
                high, low = rounded_parts(lines[coil])
                mixture = dot(zh_ref[...], high) + dot(zh_ref[...], low) + dot(zl_ref[...], high)
                line_real = mixture[:tall, :wide] - mixture[tall:, wide:]
                line_imag = mixture[:tall, wide:] + mixture[tall:, :wide]
                coil_map = maps_ref[coil].astype(jnp.float32)
                map_real, map_imag = coil_map[:, :wide], coil_map[:, wide:]
                real_part = map_real * line_real + map_imag * line_imag
                imag_part = map_real * line_imag - map_imag * line_real
                fresh = jnp.concatenate([real_part, imag_part], axis=1)
                total[...] = jnp.where(coil == 0, fresh, total[...] + fresh)

            for spot in range(count):
                slots[which, spot] = total[spot * z_count : spot * z_count + window].astype(
                    jnp.bfloat16
                )
            for step in range(1, count):
                spreading(which, step, True).start()
            parts[which, me] = slots[which, me]

        def finish_spreading(which):
            for step in range(1, count):
                spreading(which, step, False).wait_recv()
            for spot in range(slab_count):
                summed = parts[which, spot].astype(jnp.float32)
                for other in range(spot + slab_count, count, slab_count):
                    summed = summed + parts[which, other].astype(jnp.float32)
                summed = summed.astype(jnp.bfloat16).astype(jnp.float32)
                outs[which][:, 2 * spot, :] = summed[:, :wide]
                outs[which][:, 2 * spot + 1, :] = summed[:, wide:]

        start_moving(0)
        start_spreading(0)
        start_moving(1)
        finish_spreading(0)

        @pl.loop(0, z_count + 4, unroll=2)
        def _(row):
            narrow = narrow_taps(image_ref, row + 1, half_len).astype(jnp.bfloat16)
            taps_zero[row] = narrow
            pre = dot(narrow, first_ref[...])
            pre_first[row] = pre
            act = pre / (1.0 + jnp.exp(-pre))
            fill_taps(
                taps_first, row, jnp.where(row_inside(row - 2, me, z_count, length), act, 0.0)
            )

        @pl.loop(0, z_count + 2, unroll=2)
        def _(row):
            pre = conv_row(taps_first, middle_ref, row)
            pre_middle[row] = pre
            act = pre / (1.0 + jnp.exp(-pre))
            fill_taps(
                taps_middle, row, jnp.where(row_inside(row - 1, me, z_count, length), act, 0.0)
            )

        @pl.loop(0, z_count, unroll=2)
        def _(row):
            planes[row] = conv_row(taps_middle, last_ref, row).T[: 2 * slab_count]

        for spot in range(slab_count):
            for row in range(z_count):
                stacked[spot, 2 * row : 2 * row + 2] = planes[row, 2 * spot : 2 * spot + 2]
            refined_slots[spot] = stacked[spot].astype(jnp.bfloat16)
        for step in range(1, count):
            refining(step, True).start()
        refined_ref[me] = refined_slots[slab]
        start_spreading(1)
        for step in range(1, count):
            refining(step, False).wait_recv()
        finish_spreading(1)
        for which in range(2):
            for step in range(1, slab_count):
                moving(which, step, sources[which], True).wait_send()
            for step in range(1, count):
                spreading(which, step, True).wait_send()
        for step in range(1, count):
            refining(step, True).wait_send()

    def taps(extra):
        return jax.ShapeDtypeStruct((z_count + extra, half_len, 3 * LANES), jnp.bfloat16)

    def full(extra):
        return jax.ShapeDtypeStruct((z_count + extra, half_len, LANES), jnp.float32)

    shape = jax.ShapeDtypeStruct((window, 2 * slab_count, wide), jnp.float32)
    whole = pl.BlockSpec(memory_space=pltpu.VMEM)
    return pl.pallas_call(
        kernel,
        out_shape=(
            shape,
            jax.ShapeDtypeStruct((count, 2 * z_count, half_len), jnp.bfloat16),
            jax.ShapeDtypeStruct((z_count + 4, half_len, LANES), jnp.bfloat16),
            taps(4), taps(2), full(4), full(2),
        ),
        in_specs=[whole] * 10,
        out_specs=(whole,) * 7,
        scratch_shapes=[
            pltpu.VMEM((window, 2 * slab_count, wide), jnp.float32),
            pltpu.VMEM((2, slab_count, coil_count, slab_rows, width), jnp.bfloat16),
            pltpu.VMEM((coil_count, length, 2 * wide), jnp.float32),
            pltpu.VMEM((tall, 2 * wide), jnp.float32),
            pltpu.VMEM((2, count, window, 2 * wide), jnp.bfloat16),
            pltpu.VMEM((2, count, window, 2 * wide), jnp.bfloat16),
            pltpu.VMEM((z_count, 2 * slab_count, half_len), jnp.float32),
            pltpu.VMEM((slab_count, 2 * z_count, half_len), jnp.float32),
            pltpu.VMEM((slab_count, 2 * z_count, half_len), jnp.bfloat16),
            pltpu.SemaphoreType.DMA((2, slab_count)),
            pltpu.SemaphoreType.DMA((2, slab_count)),
            pltpu.SemaphoreType.DMA((2, count)),
            pltpu.SemaphoreType.DMA((2, count)),
            pltpu.SemaphoreType.DMA((count,)),
            pltpu.SemaphoreType.DMA((count,)),
        ],
        compiler_params=pltpu.CompilerParams(
            collective_id=collective_id, has_side_effects=True, vmem_limit_bytes=56 * 2**20
        ),
    )(kspace, cotangent, maps, *two_parts(table_y), *two_parts(table_z), *weights)


LANES = 128


def tap_rows(kernel):
    edge = [(0, 0), (0, 0), (0, LANES - kernel.shape[2]), (0, LANES - kernel.shape[3])]
    return jnp.pad(kernel, edge).reshape(3, 3 * LANES, LANES)


def back_taps(kernel):
    return jnp.transpose(jnp.flip(kernel, (0, 1)), (0, 1, 3, 2))


def narrow_weights(kernel):
    flat = kernel.reshape(9 * kernel.shape[2], kernel.shape[3])
    return jnp.pad(flat, ((0, LANES - flat.shape[0]), (0, 0)))


def narrow_taps(planes_ref, row, y_count):
    pieces = []
    for shift_z in range(3):
        plane = planes_ref[row + shift_z]
        width = plane.shape[1]
        position = lax.broadcasted_iota(jnp.int32, plane.shape, 1)
        pieces.append(jnp.where(position == 0, 0.0, pltpu.roll(plane, 1, 1)))
        pieces.append(plane)
        pieces.append(jnp.where(position >= y_count - 1, 0.0, pltpu.roll(plane, width - 1, 1)))
    used = 9 * planes_ref.shape[1]
    pieces.append(jnp.zeros((LANES - used, planes_ref.shape[2]), jnp.float32))
    return jnp.concatenate(pieces, axis=0).T[:y_count]


def fill_taps(taps_ref, row, values):
    y_count = values.shape[0]
    position = lax.broadcasted_iota(jnp.int32, values.shape, 0)
    before = jnp.where(position == 0, 0.0, pltpu.roll(values, 1, 0))
    after = jnp.where(position == y_count - 1, 0.0, pltpu.roll(values, y_count - 1, 0))
    taps_ref[row, :, :LANES] = before.astype(jnp.bfloat16)
    taps_ref[row, :, LANES : 2 * LANES] = values.astype(jnp.bfloat16)
    taps_ref[row, :, 2 * LANES :] = after.astype(jnp.bfloat16)


def conv_row(taps_ref, weight_ref, row):
    summed = dot(taps_ref[row], weight_ref[0])
    for shift_z in range(1, 3):
        summed = summed + dot(taps_ref[row + shift_z], weight_ref[shift_z])
    return summed


def row_inside(row, me, z_count, length):
    place = me * z_count + row
    return jnp.logical_and(place >= 0, place < length)


def backward_layers(
    adjoint, taps_zero, taps_first, taps_middle, pre_first, pre_middle, weights,
    z_count, length, y_count, x_count, slot_rows,
):
    channels = LANES // x_count
    few = adjoint.shape[1]

    def kernel(
        adjoint_ref, zero_ref, first_ref, middle_ref, pre_first_ref, pre_middle_ref,
        back_middle_ref, back_last_ref, rounded_ref, out_taps, grad_taps, sums, narrow_sums, out_ref,
    ):
        me = my_position()

        @pl.loop(0, z_count + 2, unroll=2)
        def _(row):
            narrow = (-narrow_taps(adjoint_ref, row + 2, y_count)).astype(jnp.bfloat16)
            out_taps[row] = narrow
            grad = dot(narrow, back_last_ref[...]) * silu_grad(pre_middle_ref[row])
            fill_taps(
                grad_taps, row, jnp.where(row_inside(row - 1, me, z_count, length), grad, 0.0)
            )

        sums[...] = jnp.zeros_like(sums)
        narrow_sums[...] = jnp.zeros_like(narrow_sums)

        def over_pixels(left, right):
            return lax.dot_general(
                left, right, (((0,), (0,)), ((), ())), preferred_element_type=jnp.float32
            )

        @pl.loop(0, z_count, unroll=2)
        def _(row):
            grad = conv_row(grad_taps, back_middle_ref, row) * silu_grad(pre_first_ref[row + 2])
            narrow_sums[0] += over_pixels(zero_ref[row + 2], grad.astype(jnp.bfloat16))
            narrow_sums[1] += over_pixels(
                out_taps[row + 1], middle_ref[row + 1, :, LANES : 2 * LANES]
            )
            center = grad_taps[row + 1, :, LANES : 2 * LANES]
            for shift_z in range(3):
                sums[shift_z] += over_pixels(center, first_ref[row + 1 + shift_z])

        out_ref[...] = jnp.zeros_like(out_ref)
        group = lax.broadcasted_iota(jnp.int32, (channels, LANES), 1) // channels
        for shift_z in range(3):
            for shift_y in range(3):
                tap = shift_z * 3 + shift_y
                lanes = slice(shift_y * LANES, (shift_y + 1) * LANES)
                square = sums[shift_z, :, lanes]
                folded = jnp.zeros((channels, LANES), jnp.float32)
                for shift_x in range(3):
                    picked = jnp.zeros((channels, LANES), jnp.float32)
                    for spot in range(x_count):
                        picked = picked + jnp.where(
                            group == spot + shift_x - 1,
                            square[spot * channels : (spot + 1) * channels],
                            0.0,
                        )
                    turn = LANES // 2
                    while turn >= channels:
                        picked = picked + pltpu.roll(picked, turn, 1)
                        turn //= 2
                    folded = jnp.where(group == shift_x, picked, folded)
                out_ref[tap * channels : (tap + 1) * channels] = folded
                base = 9 * channels + tap * few
                out_ref[base : base + few] = narrow_sums[0, tap * few : (tap + 1) * few]
                base = base + 9 * few
                out_ref[base : base + few] = narrow_sums[1, (8 - tap) * few : (9 - tap) * few]
        rounded_ref[...] = out_ref[...].astype(jnp.bfloat16)

    whole = pl.BlockSpec(memory_space=pltpu.VMEM)
    return pl.pallas_call(
        kernel,
        out_shape=jax.ShapeDtypeStruct((slot_rows, LANES), jnp.bfloat16),
        in_specs=[whole] * 8,
        out_specs=whole,
        scratch_shapes=[
            pltpu.VMEM((z_count + 2, y_count, LANES), jnp.bfloat16),
            pltpu.VMEM((z_count + 2, y_count, 3 * LANES), jnp.bfloat16),
            pltpu.VMEM((3, LANES, 3 * LANES), jnp.float32),
            pltpu.VMEM((2, LANES, LANES), jnp.float32),
            pltpu.VMEM((slot_rows, LANES), jnp.float32),
        ],
        compiler_params=pltpu.CompilerParams(vmem_limit_bytes=56 * 2**20),
    )(adjoint, taps_zero, taps_first, taps_middle, pre_first, pre_middle, *weights)


def band_sums(pairs, x_count):
    pieces = []
    for shift_x in range(3):
        picked = [
            pairs(target + shift_x - 1, target)
            for target in range(x_count)
            if 0 <= target + shift_x - 1 < x_count
        ]
        pieces.append(functools.reduce(jnp.add, picked))
    return jnp.stack(pieces)


def shards(
    kspace,
    measured,
    cotangent,
    coil_maps,
    sample_mask,
    step_size,
    weight_first,
    weight_middle,
    weight_last,
):
    slab_count, _, count = group_sizes()
    length = coil_maps.shape[2]
    half_len = kspace.shape[3] // 2
    z_count = length // count
    rim = 4
    lanes = slab_count * weight_middle.shape[2]
    fits = coil_maps.shape[1] == 1 and length % count == 0 and z_count % 8 == 0
    if not fits or lanes != LANES or half_len % 16 or 18 * slab_count > LANES:
        return shards_small_chunks(
            kspace,
            measured,
            cotangent,
            coil_maps,
            sample_mask,
            step_size,
            weight_first,
            weight_middle,
            weight_last,
        )
    x_count = slab_count

    kernel_middle = banded(weight_middle, x_count)
    kernel_last = banded(weight_last, x_count)
    adjoint, refined_all, *kept = images(
        kspace,
        cotangent,
        coil_maps,
        (
            narrow_weights(banded(weight_first, x_count)),
            tap_rows(kernel_middle),
            tap_rows(kernel_last),
        ),
        rim,
        0,
    )
    refined_all = refined_all.reshape(1, length, 2, half_len)

    spectra = lines_z(coil_expand(refined_all, coil_maps).astype(jnp.bfloat16), -1.0)
    spectra_slab = lax.all_to_all(
        spectra.astype(jnp.bfloat16), "slab", split_axis=2, concat_axis=1, tiled=True
    )
    model_term = lines_y(spectra_slab, -1.0)
    sampled = sample_mask.astype(jnp.float32)
    sampled = jnp.concatenate([sampled, sampled], axis=1)
    current = kspace.astype(jnp.float32)
    updated = (
        current - step_size[0] * sampled * (current - measured.astype(jnp.float32)) - model_term
    ).astype(jnp.bfloat16)

    channels = LANES // x_count
    few = 2 * x_count
    used = 9 * (channels + 2 * few)
    slot_rows = -(-used // (16 * count)) * 16 * count
    local = backward_layers(
        adjoint,
        *kept,
        (tap_rows(back_taps(kernel_middle)), narrow_weights(back_taps(kernel_last))),
        z_count,
        length,
        half_len,
        x_count,
        slot_rows,
    )
    total = total_of(local.reshape(count, -1, LANES), 3)
    total = total.reshape(slot_rows, LANES).astype(jnp.float32)
    wide_rows = 9 * channels
    middle = total[:wide_rows].reshape(3, 3, channels, x_count, channels)[:, :, :, :3]
    first = total[wide_rows : wide_rows + 9 * few].reshape(3, 3, x_count, 2, x_count, channels)
    last = total[wide_rows + 9 * few : used].reshape(3, 3, x_count, 2, x_count, channels)
    grad_middle = jnp.transpose(middle, (3, 0, 2, 1, 4))
    grad_first = band_sums(lambda source, target: first[:, :, source, :, target], x_count)
    grad_last = band_sums(lambda source, target: last[:, :, target, :, source], x_count)
    return (
        updated,
        jnp.transpose(grad_first, (0, 1, 4, 2, 3)),
        grad_middle,
        jnp.transpose(grad_last, (0, 1, 3, 2, 4)),
    )


def solution(mesh):
    return jax.shard_map(
        shards,
        mesh=mesh,
        in_specs=(
            P(("grp", "coil", "half"), None, "slab", None),
            P(("grp", "coil", "half"), None, "slab", None),
            P(("grp", "coil", "half"), None, "slab", None),
            P(("grp", "coil", "half"), "slab", None, None),
            P(("grp", "slab"), None),
            P(),
            P(),
            P(),
            P(),
        ),
        out_specs=(
            P(("grp", "coil", "half"), None, "slab", None),
            P("grp", None, None, None, None),
            P("grp", None, None, None, None),
            P("grp", None, None, None, None),
        ),
        check_vma=False,
    )
```

```python
import functools
import math

import jax
import jax.numpy as jnp
import ml_dtypes
import numpy as np
from jax import lax
from jax.experimental import pallas as pl
from jax.experimental.pallas import tpu as pltpu
from jax.sharding import PartitionSpec as P


def with_halo(block, sides, width):
    for axis, dim in sides:
        count = lax.axis_size(axis)
        forward = [(i, i + 1) for i in range(count - 1)]
        backward = [(target, source) for source, target in forward]
        low = lax.ppermute(
            lax.slice_in_dim(block, block.shape[dim] - width, None, axis=dim), axis, forward
        )
        high = lax.ppermute(lax.slice_in_dim(block, 0, width, axis=dim), axis, backward)
        block = jnp.concatenate([low, block, high], axis=dim)
    return block


def dft_parts(length):
    position = lax.iota(jnp.int32, length)
    product = position[:, None] * position[None, :] % length
    angles = product.astype(jnp.float32) * (2.0 * math.pi / length)
    factor = 1.0 / math.sqrt(length)
    return (jnp.cos(angles) * factor, jnp.sin(angles) * factor)


def plane_table(length, orient):
    cos_part, sin_part = dft_parts(length)
    upper_rows = jnp.concatenate([cos_part, orient * sin_part], axis=1)
    lower_rows = jnp.concatenate([-orient * sin_part, cos_part], axis=1)
    return jnp.concatenate([upper_rows, lower_rows], axis=0)


def along_y(values, table):
    return jnp.einsum(
        "cxzk,kw->cxzw",
        values,
        table,
        precision=lax.Precision.HIGH,
        preferred_element_type=jnp.float32,
    )


def along_z(values, orient):
    length = values.shape[2]
    half_len = values.shape[3] // 2
    cos_part, sin_part = dft_parts(length)
    stacked = jnp.concatenate([cos_part, sin_part], axis=0)
    mixture = jnp.einsum(
        "wz,cxzk->cxwk",
        stacked,
        values,
        precision=lax.Precision.HIGH,
        preferred_element_type=jnp.float32,
    )
    direct = mixture[:, :, :length]
    crossed = mixture[:, :, length:]
    turned = jnp.concatenate(
        [-orient * crossed[..., half_len:], orient * crossed[..., :half_len]], axis=-1
    )
    return direct + turned


def coil_adjoint(lines, coil_maps):
    half_len = lines.shape[3] // 2
    map_values = coil_maps.astype(jnp.float32)
    map_real = map_values[..., :half_len]
    map_imag = map_values[..., half_len:]
    line_real = lines[..., :half_len]
    line_imag = lines[..., half_len:]
    real_sum = jnp.sum(map_real * line_real + map_imag * line_imag, axis=0)
    imag_sum = jnp.sum(map_real * line_imag - map_imag * line_real, axis=0)
    return jnp.stack([real_sum, imag_sum], axis=2)


def coil_expand(image, coil_maps):
    half_len = coil_maps.shape[3] // 2
    map_values = coil_maps.astype(jnp.float32)
    map_real = map_values[..., :half_len]
    map_imag = map_values[..., half_len:]
    image_real = image[:, :, 0].astype(jnp.float32)
    image_imag = image[:, :, 1].astype(jnp.float32)
    out_real = map_real * image_real - map_imag * image_imag
    out_imag = map_real * image_imag + map_imag * image_real
    return jnp.concatenate([out_real, out_imag], axis=-1)


def with_rims(values):
    return with_halo(values, (("slab", 0), (("coil", "half"), 1)), 1)


def columns_of(padded):
    y_count = padded.shape[3]
    widened = jnp.pad(padded, ((0, 0), (0, 0), (0, 0), (1, 1)))
    return jnp.concatenate(
        [widened[..., shift_y : shift_y + y_count] for shift_y in range(3)], axis=2
    )


def conv_apply(columns, matrix):
    x_count = columns.shape[0] - 2
    z_count = columns.shape[1] - 2
    summed = None
    for shift_x in range(3):
        for shift_z in range(3):
            partial_sum = jnp.einsum(
                "ok,xzky->xzoy",
                matrix[shift_x, shift_z],
                columns[shift_x : shift_x + x_count, shift_z : shift_z + z_count],
                preferred_element_type=jnp.float32,
            )
            summed = partial_sum if summed is None else summed + partial_sum
    return summed


def weight_grad(out_grad, columns):
    x_count = out_grad.shape[0]
    z_count = out_grad.shape[1]
    outer_list = []
    for shift_x in range(3):
        inner_list = []
        for shift_z in range(3):
            inner_list.append(
                jnp.einsum(
                    "xzoy,xzky->ok",
                    out_grad,
                    columns[shift_x : shift_x + x_count, shift_z : shift_z + z_count],
                    preferred_element_type=jnp.float32,
                )
            )
        outer_list.append(jnp.stack(inner_list, axis=0))
    return jnp.stack(outer_list, axis=0)


def as_matrix(weight):
    return weight.reshape(3, 3, weight.shape[2], 3 * weight.shape[4])


def flipped(weight):
    turned = jnp.transpose(jnp.flip(weight, (0, 1, 3)), (0, 1, 4, 3, 2))
    return turned.reshape(3, 3, weight.shape[4], 3 * weight.shape[2])


def silu_grad(values):
    sigma = jax.nn.sigmoid(values)
    return sigma * (1.0 + values * (1.0 - sigma))


def shards_small_chunks(
    kspace,
    measured,
    cotangent,
    coil_maps,
    sample_mask,
    step_size,
    weight_first,
    weight_middle,
    weight_last,
):
    half_len = kspace.shape[3] // 2
    inverse_y = plane_table(half_len, 1.0)
    k_moved, g_moved = (
        lax.all_to_all(kspace, "slab", split_axis=1, concat_axis=2, tiled=True),
        lax.all_to_all(cotangent, "slab", split_axis=1, concat_axis=2, tiled=True),
    )
    k_lines = along_y(k_moved.astype(jnp.float32), inverse_y)
    g_lines = along_y(g_moved.astype(jnp.float32), inverse_y)
    image_full = coil_adjoint(along_z(k_lines, 1.0), coil_maps)
    adjoint_full = coil_adjoint(along_z(g_lines, 1.0), coil_maps)
    summed_image, summed_adjoint = lax.psum((image_full, adjoint_full), ("coil", "half"))
    z_count = summed_image.shape[1] // lax.axis_size(("coil", "half"))
    start = lax.axis_index(("coil", "half")) * z_count
    image = lax.dynamic_slice_in_dim(summed_image, start, z_count, 1)
    adjoint = lax.dynamic_slice_in_dim(summed_adjoint, start, z_count, 1)
    layer_zero = image.astype(jnp.bfloat16)
    cols_zero = columns_of(with_rims(layer_zero))
    pre_first = conv_apply(cols_zero, as_matrix(weight_first))
    act_first = jax.nn.silu(pre_first).astype(jnp.bfloat16)
    cols_first = columns_of(with_rims(act_first))
    pre_middle = conv_apply(cols_first, as_matrix(weight_middle))
    act_middle = jax.nn.silu(pre_middle).astype(jnp.bfloat16)
    cols_middle = columns_of(with_rims(act_middle))
    refined = conv_apply(cols_middle, as_matrix(weight_last)).astype(jnp.bfloat16)
    refined_all = lax.all_gather(refined, ("coil", "half"), axis=1, tiled=True)
    spectra_lines = along_z(coil_expand(refined_all, coil_maps), -1.0)
    spectra_slab = lax.all_to_all(
        spectra_lines.astype(jnp.bfloat16), "slab", split_axis=2, concat_axis=1, tiled=True
    ).astype(spectra_lines.dtype)
    model_term = along_y(spectra_slab, plane_table(half_len, -1.0))
    sampled = sample_mask.astype(jnp.float32)
    sampled = jnp.concatenate([sampled, sampled], axis=1)
    current = kspace.astype(jnp.float32)
    updated = (
        current - step_size[0] * sampled * (current - measured.astype(jnp.float32)) - model_term
    ).astype(jnp.bfloat16)
    grad_out = (-adjoint).astype(jnp.bfloat16)
    grad_last = weight_grad(grad_out, cols_middle)
    back_middle = conv_apply(columns_of(with_rims(grad_out)), flipped(weight_last))
    grad_pre_middle = (back_middle * silu_grad(pre_middle)).astype(jnp.bfloat16)
    grad_middle = weight_grad(grad_pre_middle, cols_first)
    back_first = conv_apply(columns_of(with_rims(grad_pre_middle)), flipped(weight_middle))
    grad_pre_first = (back_first * silu_grad(pre_first)).astype(jnp.bfloat16)
    grad_first = weight_grad(grad_pre_first, cols_zero)
    grad_first, grad_middle, grad_last = lax.psum(
        (grad_first, grad_middle, grad_last), ("slab", "coil", "half")
    )
    return (
        updated,
        grad_first.reshape(weight_first.shape),
        grad_middle.reshape(weight_middle.shape),
        grad_last.reshape(weight_last.shape),
    )


GROUP = ("coil", "half", "slab")


def group_sizes():
    return lax.axis_size("slab"), lax.axis_size("half"), lax.axis_size(GROUP)


def my_position():
    slab_count, half_count, _ = group_sizes()
    coil_half = lax.axis_index("coil") * half_count + lax.axis_index("half")
    return coil_half * slab_count + lax.axis_index("slab")


def device_at(position):
    slab_count, half_count, _ = group_sizes()
    coil_half = lax.div(position, slab_count)
    return {
        "slab": lax.rem(position, slab_count),
        "coil": lax.div(coil_half, half_count),
        "half": lax.rem(coil_half, half_count),
    }


def greet(count, me):
    barrier = pltpu.get_barrier_semaphore()
    for step in range(1, count):
        peer = lax.rem(me + step, count)
        pl.semaphore_signal(
            barrier, inc=1, device_id=device_at(peer), device_id_type=pl.DeviceIdType.MESH
        )
    pl.semaphore_wait(barrier, count - 1)


def send_to(src, dst, send_sem, recv_sem, peer):
    return pltpu.make_async_remote_copy(
        src_ref=src,
        dst_ref=dst,
        send_sem=send_sem,
        recv_sem=recv_sem,
        device_id=device_at(peer),
        device_id_type=pl.DeviceIdType.MESH,
    )


def scatter_slots(count, me, pick, src_ref, dst_ref, send_sem, recv_sem):
    copies = []
    for step in range(1, count):
        peer = lax.rem(me + step, count)
        copy = send_to(
            src_ref.at[pick(peer)], dst_ref.at[me], send_sem.at[step], recv_sem.at[step], peer
        )
        copy.start()
        copies.append(copy)
    dst_ref[me] = src_ref[pick(me)]
    for step in range(1, count):
        source = lax.rem(me + count - step, count)
        send_to(
            src_ref.at[pick(source)],
            dst_ref.at[source],
            send_sem.at[step],
            recv_sem.at[step],
            source,
        ).wait_recv()
    for copy in copies:
        copy.wait_send()


def total_of(values, collective_id):
    _, _, count = group_sizes()

    def kernel(src_ref, dst_ref, parts, own, send_sem, recv_sem, send_two, recv_two):
        me = my_position()
        greet(count, me)
        scatter_slots(count, me, lambda peer: peer, src_ref, parts, send_sem, recv_sem)
        own[0] = jnp.sum(parts[...].astype(jnp.float32), axis=0).astype(own.dtype)
        scatter_slots(count, me, lambda peer: 0, own, dst_ref, send_two, recv_two)

    semaphores = pltpu.SemaphoreType.DMA((count,))
    return pl.pallas_call(
        kernel,
        out_shape=jax.ShapeDtypeStruct(values.shape, values.dtype),
        in_specs=[pl.BlockSpec(memory_space=pltpu.VMEM)],
        out_specs=pl.BlockSpec(memory_space=pltpu.VMEM),
        scratch_shapes=[
            pltpu.VMEM(values.shape, values.dtype),
            pltpu.VMEM((1,) + values.shape[1:], values.dtype),
            semaphores,
            semaphores,
            semaphores,
            semaphores,
        ],
        compiler_params=pltpu.CompilerParams(collective_id=collective_id, has_side_effects=True),
    )(values)


def dft_constants(length):
    position = np.arange(length)
    angles = (position[:, None] * position[None, :] % length) * (2.0 * math.pi / length)
    factor = 1.0 / math.sqrt(length)
    return np.cos(angles) * factor, np.sin(angles) * factor


def plane_constant(length, orient):
    cos_part, sin_part = dft_constants(length)
    return jnp.asarray(
        np.block([[cos_part, orient * sin_part], [-orient * sin_part, cos_part]]), jnp.bfloat16
    )


def lines_y(values, orient):
    return jnp.einsum(
        "cxzk,kw->cxzw",
        values,
        plane_constant(values.shape[3] // 2, orient),
        preferred_element_type=jnp.float32,
    )


def lines_z(values, orient):
    length = values.shape[2]
    half_len = values.shape[3] // 2
    cos_part, sin_part = dft_constants(length)
    mixture = jnp.einsum(
        "wz,cxzk->cxwk",
        jnp.asarray(np.concatenate([cos_part, sin_part], axis=0), jnp.bfloat16),
        values,
        preferred_element_type=jnp.float32,
    )
    direct = mixture[:, :, :length]
    crossed = mixture[:, :, length:]
    turned = jnp.concatenate(
        [-orient * crossed[..., half_len:], orient * crossed[..., :half_len]], axis=-1
    )
    return direct + turned


def band_of(x_count):
    shift = np.arange(3)[:, None, None]
    source = np.arange(x_count)[None, :, None]
    target = np.arange(x_count)[None, None, :]
    return (source == target + shift - 1).astype(np.float32)


def banded(weight, x_count):
    band = jnp.asarray(band_of(x_count), jnp.bfloat16)
    wide = jnp.einsum("dzoyi,dab->zyaibo", weight, band, preferred_element_type=jnp.bfloat16)
    return wide.reshape(3, 3, x_count * weight.shape[4], x_count * weight.shape[2])


def halves_padded(values, wide):
    half_len = values.shape[-1] // 2
    edge = [(0, 0)] * (values.ndim - 1) + [(0, wide - half_len)]
    return jnp.concatenate(
        [jnp.pad(values[..., :half_len], edge), jnp.pad(values[..., half_len:], edge)], axis=-1
    )


def two_parts(table):
    high = table.astype(ml_dtypes.bfloat16)
    low = (table - high.astype(np.float64)).astype(ml_dtypes.bfloat16)
    return jnp.asarray(high), jnp.asarray(low)


def rounded_parts(values):
    high = values.astype(jnp.bfloat16)
    return high, (values - high.astype(jnp.float32)).astype(jnp.bfloat16)


def dot(left, right):
    return jnp.dot(left, right, preferred_element_type=jnp.float32)


def images(kspace, cotangent, coil_maps, weights, rim, collective_id):
    slab_count, _, count = group_sizes()
    coil_count, x_count, slab_rows, width = kspace.shape
    length = slab_count * slab_rows
    half_len = width // 2
    wide = -(-half_len // 128) * 128
    z_count = length // count
    window = z_count + 2 * rim
    tall = length + 2 * rim

    cos_y, sin_y = dft_constants(half_len)
    table_y = np.zeros((width, 2 * wide))
    table_y[:half_len, :half_len] = cos_y
    table_y[:half_len, wide : wide + half_len] = sin_y
    table_y[half_len:, :half_len] = -sin_y
    table_y[half_len:, wide : wide + half_len] = cos_y
    cos_z, sin_z = dft_constants(length)
    table_z = np.zeros((2 * tall, length))
    table_z[rim : rim + length] = cos_z
    table_z[tall + rim : tall + rim + length] = sin_z
    maps = halves_padded(coil_maps[:, 0], wide)
    maps = jnp.pad(maps, ((0, 0), (rim, rim), (0, 0)))

    def kernel(
        k_ref, g_ref, maps_ref, yh_ref, yl_ref, zh_ref, zl_ref, first_ref, middle_ref, last_ref,
        adjoint_ref, refined_ref, taps_zero, taps_first, taps_middle, pre_first, pre_middle,
        image_ref, moved, lines, total, slots, parts, planes, stacked, refined_slots,
        send_one, recv_one, send_two, recv_two, send_three, recv_three,
    ):
        me = my_position()
        slab = lax.axis_index("slab")
        greet(count, me)

        def moving(which, step, source_ref, sending):
            offset = step if sending else slab_count - step
            peer = lax.rem(slab + offset, slab_count)
            return pltpu.make_async_remote_copy(
                src_ref=source_ref.at[:, peer],
                dst_ref=moved.at[which, slab if sending else peer],
                send_sem=send_one.at[which, step],
                recv_sem=recv_one.at[which, step],
                device_id={"slab": peer},
                device_id_type=pl.DeviceIdType.MESH,
            )

        def spreading(which, step, sending):
            peer = lax.rem(me + (step if sending else count - step), count)
            return send_to(
                slots.at[which, peer],
                parts.at[which, me if sending else peer],
                send_two.at[which, step],
                recv_two.at[which, step],
                peer,
            )

        sources = (k_ref, g_ref)
        outs = (image_ref, adjoint_ref)

        def refining(step, sending):
            peer = lax.rem(me + (step if sending else count - step), count)
            return send_to(
                refined_slots.at[lax.rem(peer, slab_count)],
                refined_ref.at[me if sending else peer],
                send_three.at[step],
                recv_three.at[step],
                peer,
            )

        def start_moving(which):
            for step in range(1, slab_count):
                moving(which, step, sources[which], True).start()
            moved[which, slab] = sources[which][:, slab]

        def start_spreading(which):
            for step in range(1, slab_count):
                moving(which, step, sources[which], False).wait_recv()
            if which == 0:
                start_moving(1)
            for block in range(slab_count):
                rows = moved[which, block].reshape(coil_count * slab_rows, width)
                product = dot(rows, yh_ref[...]) + dot(rows, yl_ref[...])
                lines[:, block * slab_rows : (block + 1) * slab_rows] = product.reshape(
                    coil_count, slab_rows, 2 * wide
                )

            @pl.loop(0, coil_count)
            def _(coil):
                high, low = rounded_parts(lines[coil])
                mixture = dot(zh_ref[...], high) + dot(zh_ref[...], low) + dot(zl_ref[...], high)
                line_real = mixture[:tall, :wide] - mixture[tall:, wide:]
                line_imag = mixture[:tall, wide:] + mixture[tall:, :wide]
                coil_map = maps_ref[coil].astype(jnp.float32)
                map_real, map_imag = coil_map[:, :wide], coil_map[:, wide:]
                real_part = map_real * line_real + map_imag * line_imag
                imag_part = map_real * line_imag - map_imag * line_real
                fresh = jnp.concatenate([real_part, imag_part], axis=1)
                total[...] = jnp.where(coil == 0, fresh, total[...] + fresh)

            for spot in range(count):
                slots[which, spot] = total[spot * z_count : spot * z_count + window].astype(
                    jnp.bfloat16
                )
            for step in range(1, count):
                spreading(which, step, True).start()
            parts[which, me] = slots[which, me]

        def finish_spreading(which):
            for step in range(1, count):
                spreading(which, step, False).wait_recv()
            for spot in range(slab_count):
                summed = parts[which, spot].astype(jnp.float32)
                for other in range(spot + slab_count, count, slab_count):
                    summed = summed + parts[which, other].astype(jnp.float32)
                summed = summed.astype(jnp.bfloat16).astype(jnp.float32)
                outs[which][:, 2 * spot, :] = summed[:, :wide]
                outs[which][:, 2 * spot + 1, :] = summed[:, wide:]

        start_moving(0)
        start_spreading(0)
        start_spreading(1)
        finish_spreading(0)

        @pl.loop(0, z_count + 4, unroll=2)
        def _(row):
            narrow = narrow_taps(image_ref, row + 1, half_len).astype(jnp.bfloat16)
            taps_zero[row] = narrow
            pre = dot(narrow, first_ref[...])
            pre_first[row] = pre
            act = pre / (1.0 + jnp.exp(-pre))
            fill_taps(
                taps_first, row, jnp.where(row_inside(row - 2, me, z_count, length), act, 0.0)
            )

        @pl.loop(0, z_count + 2, unroll=2)
        def _(row):
            pre = conv_row(taps_first, middle_ref, row)
            pre_middle[row] = pre
            act = pre / (1.0 + jnp.exp(-pre))
            fill_taps(
                taps_middle, row, jnp.where(row_inside(row - 1, me, z_count, length), act, 0.0)
            )

        @pl.loop(0, z_count, unroll=2)
        def _(row):
            planes[row] = conv_row(taps_middle, last_ref, row).T[: 2 * slab_count]

        for spot in range(slab_count):
            for row in range(z_count):
                stacked[spot, 2 * row : 2 * row + 2] = planes[row, 2 * spot : 2 * spot + 2]
            refined_slots[spot] = stacked[spot].astype(jnp.bfloat16)
        for step in range(1, count):
            refining(step, True).start()
        refined_ref[me] = refined_slots[slab]
        for step in range(1, count):
            refining(step, False).wait_recv()
        finish_spreading(1)
        for which in range(2):
            for step in range(1, slab_count):
                moving(which, step, sources[which], True).wait_send()
            for step in range(1, count):
                spreading(which, step, True).wait_send()
        for step in range(1, count):
            refining(step, True).wait_send()

    def taps(extra):
        return jax.ShapeDtypeStruct((z_count + extra, half_len, 3 * LANES), jnp.bfloat16)

    def full(extra):
        return jax.ShapeDtypeStruct((z_count + extra, half_len, LANES), jnp.float32)

    shape = jax.ShapeDtypeStruct((window, 2 * slab_count, wide), jnp.float32)
    whole = pl.BlockSpec(memory_space=pltpu.VMEM)
    return pl.pallas_call(
        kernel,
        out_shape=(
            shape,
            jax.ShapeDtypeStruct((count, 2 * z_count, half_len), jnp.bfloat16),
            jax.ShapeDtypeStruct((z_count + 4, half_len, LANES), jnp.bfloat16),
            taps(4), taps(2), full(4), full(2),
        ),
        in_specs=[whole] * 10,
        out_specs=(whole,) * 7,
        scratch_shapes=[
            pltpu.VMEM((window, 2 * slab_count, wide), jnp.float32),
            pltpu.VMEM((2, slab_count, coil_count, slab_rows, width), jnp.bfloat16),
            pltpu.VMEM((coil_count, length, 2 * wide), jnp.float32),
            pltpu.VMEM((tall, 2 * wide), jnp.float32),
            pltpu.VMEM((2, count, window, 2 * wide), jnp.bfloat16),
            pltpu.VMEM((2, count, window, 2 * wide), jnp.bfloat16),
            pltpu.VMEM((z_count, 2 * slab_count, half_len), jnp.float32),
            pltpu.VMEM((slab_count, 2 * z_count, half_len), jnp.float32),
            pltpu.VMEM((slab_count, 2 * z_count, half_len), jnp.bfloat16),
            pltpu.SemaphoreType.DMA((2, slab_count)),
            pltpu.SemaphoreType.DMA((2, slab_count)),
            pltpu.SemaphoreType.DMA((2, count)),
            pltpu.SemaphoreType.DMA((2, count)),
            pltpu.SemaphoreType.DMA((count,)),
            pltpu.SemaphoreType.DMA((count,)),
        ],
        compiler_params=pltpu.CompilerParams(
            collective_id=collective_id, has_side_effects=True, vmem_limit_bytes=56 * 2**20
        ),
    )(kspace, cotangent, maps, *two_parts(table_y), *two_parts(table_z), *weights)


LANES = 128


def tap_rows(kernel):
    edge = [(0, 0), (0, 0), (0, LANES - kernel.shape[2]), (0, LANES - kernel.shape[3])]
    return jnp.pad(kernel, edge).reshape(3, 3 * LANES, LANES)


def back_taps(kernel):
    return jnp.transpose(jnp.flip(kernel, (0, 1)), (0, 1, 3, 2))


def narrow_weights(kernel):
    flat = kernel.reshape(9 * kernel.shape[2], kernel.shape[3])
    return jnp.pad(flat, ((0, LANES - flat.shape[0]), (0, 0)))


def narrow_taps(planes_ref, row, y_count):
    pieces = []
    for shift_z in range(3):
        plane = planes_ref[row + shift_z]
        width = plane.shape[1]
        position = lax.broadcasted_iota(jnp.int32, plane.shape, 1)
        pieces.append(jnp.where(position == 0, 0.0, pltpu.roll(plane, 1, 1)))
        pieces.append(plane)
        pieces.append(jnp.where(position >= y_count - 1, 0.0, pltpu.roll(plane, width - 1, 1)))
    used = 9 * planes_ref.shape[1]
    pieces.append(jnp.zeros((LANES - used, planes_ref.shape[2]), jnp.float32))
    return jnp.concatenate(pieces, axis=0).T[:y_count]


def fill_taps(taps_ref, row, values):
    y_count = values.shape[0]
    position = lax.broadcasted_iota(jnp.int32, values.shape, 0)
    before = jnp.where(position == 0, 0.0, pltpu.roll(values, 1, 0))
    after = jnp.where(position == y_count - 1, 0.0, pltpu.roll(values, y_count - 1, 0))
    taps_ref[row, :, :LANES] = before.astype(jnp.bfloat16)
    taps_ref[row, :, LANES : 2 * LANES] = values.astype(jnp.bfloat16)
    taps_ref[row, :, 2 * LANES :] = after.astype(jnp.bfloat16)


def conv_row(taps_ref, weight_ref, row):
    summed = dot(taps_ref[row], weight_ref[0])
    for shift_z in range(1, 3):
        summed = summed + dot(taps_ref[row + shift_z], weight_ref[shift_z])
    return summed


def row_inside(row, me, z_count, length):
    place = me * z_count + row
    return jnp.logical_and(place >= 0, place < length)


def backward_layers(
    adjoint, taps_zero, taps_first, taps_middle, pre_first, pre_middle, weights,
    z_count, length, y_count, x_count, slot_rows,
):
    channels = LANES // x_count
    few = adjoint.shape[1]

    def kernel(
        adjoint_ref, zero_ref, first_ref, middle_ref, pre_first_ref, pre_middle_ref,
        back_middle_ref, back_last_ref, rounded_ref, out_taps, grad_taps, sums, narrow_sums, out_ref,
    ):
        me = my_position()

        @pl.loop(0, z_count + 2, unroll=2)
        def _(row):
            narrow = (-narrow_taps(adjoint_ref, row + 2, y_count)).astype(jnp.bfloat16)
            out_taps[row] = narrow
            grad = dot(narrow, back_last_ref[...]) * silu_grad(pre_middle_ref[row])
            fill_taps(
                grad_taps, row, jnp.where(row_inside(row - 1, me, z_count, length), grad, 0.0)
            )

        sums[...] = jnp.zeros_like(sums)
        narrow_sums[...] = jnp.zeros_like(narrow_sums)

        def over_pixels(left, right):
            return lax.dot_general(
                left, right, (((0,), (0,)), ((), ())), preferred_element_type=jnp.float32
            )

        @pl.loop(0, z_count, unroll=2)
        def _(row):
            grad = conv_row(grad_taps, back_middle_ref, row) * silu_grad(pre_first_ref[row + 2])
            narrow_sums[0] += over_pixels(zero_ref[row + 2], grad.astype(jnp.bfloat16))
            narrow_sums[1] += over_pixels(
                out_taps[row + 1], middle_ref[row + 1, :, LANES : 2 * LANES]
            )
            center = grad_taps[row + 1, :, LANES : 2 * LANES]
            for shift_z in range(3):
                sums[shift_z] += over_pixels(center, first_ref[row + 1 + shift_z])

        out_ref[...] = jnp.zeros_like(out_ref)
        group = lax.broadcasted_iota(jnp.int32, (channels, LANES), 1) // channels
        for shift_z in range(3):
            for shift_y in range(3):
                tap = shift_z * 3 + shift_y
                lanes = slice(shift_y * LANES, (shift_y + 1) * LANES)
                square = sums[shift_z, :, lanes]
                folded = jnp.zeros((channels, LANES), jnp.float32)
                for shift_x in range(3):
                    picked = jnp.zeros((channels, LANES), jnp.float32)
                    for spot in range(x_count):
                        picked = picked + jnp.where(
                            group == spot + shift_x - 1,
                            square[spot * channels : (spot + 1) * channels],
                            0.0,
                        )
                    turn = LANES // 2
                    while turn >= channels:
                        picked = picked + pltpu.roll(picked, turn, 1)
                        turn //= 2
                    folded = jnp.where(group == shift_x, picked, folded)
                out_ref[tap * channels : (tap + 1) * channels] = folded
                base = 9 * channels + tap * few
                out_ref[base : base + few] = narrow_sums[0, tap * few : (tap + 1) * few]
                base = base + 9 * few
                out_ref[base : base + few] = narrow_sums[1, (8 - tap) * few : (9 - tap) * few]
        rounded_ref[...] = out_ref[...].astype(jnp.bfloat16)

    whole = pl.BlockSpec(memory_space=pltpu.VMEM)
    return pl.pallas_call(
        kernel,
        out_shape=jax.ShapeDtypeStruct((slot_rows, LANES), jnp.bfloat16),
        in_specs=[whole] * 8,
        out_specs=whole,
        scratch_shapes=[
            pltpu.VMEM((z_count + 2, y_count, LANES), jnp.bfloat16),
            pltpu.VMEM((z_count + 2, y_count, 3 * LANES), jnp.bfloat16),
            pltpu.VMEM((3, LANES, 3 * LANES), jnp.float32),
            pltpu.VMEM((2, LANES, LANES), jnp.float32),
            pltpu.VMEM((slot_rows, LANES), jnp.float32),
        ],
        compiler_params=pltpu.CompilerParams(vmem_limit_bytes=56 * 2**20),
    )(adjoint, taps_zero, taps_first, taps_middle, pre_first, pre_middle, *weights)


def band_sums(pairs, x_count):
    pieces = []
    for shift_x in range(3):
        picked = [
            pairs(target + shift_x - 1, target)
            for target in range(x_count)
            if 0 <= target + shift_x - 1 < x_count
        ]
        pieces.append(functools.reduce(jnp.add, picked))
    return jnp.stack(pieces)


def shards(
    kspace,
    measured,
    cotangent,
    coil_maps,
    sample_mask,
    step_size,
    weight_first,
    weight_middle,
    weight_last,
):
    slab_count, _, count = group_sizes()
    length = coil_maps.shape[2]
    half_len = kspace.shape[3] // 2
    z_count = length // count
    rim = 4
    lanes = slab_count * weight_middle.shape[2]
    fits = coil_maps.shape[1] == 1 and length % count == 0 and z_count % 8 == 0
    if not fits or lanes != LANES or half_len % 16 or 18 * slab_count > LANES:
        return shards_small_chunks(
            kspace,
            measured,
            cotangent,
            coil_maps,
            sample_mask,
            step_size,
            weight_first,
            weight_middle,
            weight_last,
        )
    x_count = slab_count

    kernel_middle = banded(weight_middle, x_count)
    kernel_last = banded(weight_last, x_count)
    adjoint, refined_all, *kept = images(
        kspace,
        cotangent,
        coil_maps,
        (
            narrow_weights(banded(weight_first, x_count)),
            tap_rows(kernel_middle),
            tap_rows(kernel_last),
        ),
        rim,
        0,
    )
    refined_all = refined_all.reshape(1, length, 2, half_len)

    spectra = lines_z(coil_expand(refined_all, coil_maps).astype(jnp.bfloat16), -1.0)
    spectra_slab = lax.all_to_all(
        spectra.astype(jnp.bfloat16), "slab", split_axis=2, concat_axis=1, tiled=True
    )
    model_term = lines_y(spectra_slab, -1.0)
    sampled = sample_mask.astype(jnp.float32)
    sampled = jnp.concatenate([sampled, sampled], axis=1)
    current = kspace.astype(jnp.float32)
    updated = (
        current - step_size[0] * sampled * (current - measured.astype(jnp.float32)) - model_term
    ).astype(jnp.bfloat16)

    channels = LANES // x_count
    few = 2 * x_count
    used = 9 * (channels + 2 * few)
    slot_rows = -(-used // (16 * count)) * 16 * count
    local = backward_layers(
        adjoint,
        *kept,
        (tap_rows(back_taps(kernel_middle)), narrow_weights(back_taps(kernel_last))),
        z_count,
        length,
        half_len,
        x_count,
        slot_rows,
    )
    total = total_of(local.reshape(count, -1, LANES), 3)
    total = total.reshape(slot_rows, LANES).astype(jnp.float32)
    wide_rows = 9 * channels
    middle = total[:wide_rows].reshape(3, 3, channels, x_count, channels)[:, :, :, :3]
    first = total[wide_rows : wide_rows + 9 * few].reshape(3, 3, x_count, 2, x_count, channels)
    last = total[wide_rows + 9 * few : used].reshape(3, 3, x_count, 2, x_count, channels)
    grad_middle = jnp.transpose(middle, (3, 0, 2, 1, 4))
    grad_first = band_sums(lambda source, target: first[:, :, source, :, target], x_count)
    grad_last = band_sums(lambda source, target: last[:, :, target, :, source], x_count)
    return (
        updated,
        jnp.transpose(grad_first, (0, 1, 4, 2, 3)),
        grad_middle,
        jnp.transpose(grad_last, (0, 1, 3, 2, 4)),
    )


def solution(mesh):
    return jax.shard_map(
        shards,
        mesh=mesh,
        in_specs=(
            P(("grp", "coil", "half"), None, "slab", None),
            P(("grp", "coil", "half"), None, "slab", None),
            P(("grp", "coil", "half"), None, "slab", None),
            P(("grp", "coil", "half"), "slab", None, None),
            P(("grp", "slab"), None),
            P(),
            P(),
            P(),
            P(),
        ),
        out_specs=(
            P(("grp", "coil", "half"), None, "slab", None),
            P("grp", None, None, None, None),
            P("grp", None, None, None, None),
            P("grp", None, None, None, None),
        ),
        check_vma=False,
    )
```
